512 devices in a mesh: gx: 16 (over y, x), depth: 32 (over z, core).
Axes of the slice: x: 4, y: 4, z: 16, core: 2. Of those that a mesh axis runs over, the one named last changes fastest.
Arguments:
- volume: float32 [4, 256, 32, 2048], P(None, 'depth', None, 'gx'), may hold values from -16 to 16
- extinction: float32 [128], replicated, may hold values from 0.05 to 50
- palette: float32 [16, 3], replicated, may hold values from 0.2 to 1.5
- palette_index: int32 [128], replicated, may hold values from 0 to 15
Outputs:
- image: float32 [4, 16, 4096], P(None, 'gx', 'depth')
The draws below stay inside these ranges and needn't reach their ends.
All inputs are finite; a program needn't handle non-finite values.
Results may differ from the reference program's by a relative error of at most 0.0003.
Values sent between devices are 32-bit elements; how exact they have to be, the bound alone decides.
A program may use at most 64 MiB of HBM per device.

```python
import math
import jax
import jax.numpy as jnp
from jax import lax

VARS = 4
TF = 128
PAL = 16
CX = 128
HEIGHT = 32
NX = 2048
NZ = 256
N_GX = 16


def set_ends(values, key, least, largest):
    place = [jax.random.randint(jax.random.fold_in(key, axis), (), 0, length) for axis, length in enumerate(values.shape)]
    main_axis = values.shape.index(max(values.shape))
    next_to = place[:main_axis] + [(place[main_axis] + 1) % values.shape[main_axis]] + place[main_axis + 1:]
    return values.at[tuple(place)].set(least).at[tuple(next_to)].set(largest)


def levels(rng, shape, split, low, largest):
    gain = 1.0
    for axis_at, blocks in split:
        steps = jax.random.uniform(jax.random.fold_in(jax.random.fold_in(rng, 6), axis_at), (blocks,), jnp.float32, low / len(split), largest / len(split))
        gain = gain * jnp.repeat(jnp.exp(steps), shape[axis_at] // blocks).reshape((-1,) + (1,) * (len(shape) - 1 - axis_at))
    return gain


def centred(stream_key, extent, deviation, reach, shards=(), kind=jnp.bfloat16):
    gain = levels(stream_key, extent, shards, -0.22, 0.18) if shards else 1.0
    array = jax.random.normal(stream_key, extent, jnp.float32) * deviation * gain
    return jnp.minimum(jnp.maximum(array, -reach), reach).astype(kind)


def setup_inputs(seed: int = 0) -> dict:
    arg_keys = jax.random.split(jax.random.key(seed), 5)
    return {
        "volume": centred(arg_keys[0], (VARS, NZ, HEIGHT, NX), 3.0, 16.0, ((1, 32), (3, 16)), jnp.float32),
        "extinction": jnp.clip(jnp.exp(jax.random.uniform(arg_keys[1], (TF,), jnp.float32, math.log(0.05), math.log(50.0))), 0.05, 50.0),
        "palette": jnp.clip(jax.random.uniform(arg_keys[2], (PAL, 3), jnp.float32, 0.2, 1.5), 0.2, 1.5),
        "palette_index": set_ends(jax.random.randint(arg_keys[3], (TF,), 0, PAL), jax.random.fold_in(arg_keys[3], 1), 0, PAL - 1).astype(jnp.int32),
    }


TAPS = (0.0625, 0.25, 0.375, 0.25, 0.0625)
LIGHT = (0.64, 0.6, 0.48)


def smooth_valid(values, along):
    length = values.shape[along] - 4
    result = TAPS[0] * lax.slice_in_dim(values, 0, length, axis=along)
    for offset in range(1, 5):
        result = result + TAPS[offset] * lax.slice_in_dim(values, offset, offset + length, axis=along)
    return result


def smooth_zero(values, along):
    widths = [(0, 0)] * values.ndim
    widths[along] = (2, 2)
    return smooth_valid(jnp.pad(values, widths), along)


def gradients(fields):
    centre = fields[:, 1:-1, :, 1:-1]
    grad_z = 0.5 * (fields[:, 2:, :, 1:-1] - fields[:, :-2, :, 1:-1])
    grad_x = 0.5 * (fields[:, 1:-1, :, 2:] - fields[:, 1:-1, :, :-2])
    padded = jnp.pad(centre, ((0, 0), (0, 0), (1, 1), (0, 0)))
    grad_y = 0.5 * (padded[:, :, 2:] - padded[:, :, :-2])
    return grad_z, grad_y, grad_x


def table_lookup(tables, position):
    entries = tables.shape[1]
    stops = jnp.arange(entries, dtype=position.dtype)

    def one_layer(layer):
        hats = jnp.maximum(0.0, 1.0 - jnp.abs(layer[None, :, :] - stops[:, None, None]))
        return jnp.einsum("tk,kyx->tyx", tables, hats, precision=lax.Precision.HIGHEST)

    stacked = lax.map(one_layer, position)
    return jnp.moveaxis(stacked, 1, 0)


def emission_terms(centre, fields, extinction, colors, step_len):
    grad_z, grad_y, grad_x = gradients(fields)
    facing = LIGHT[0] * grad_z[0] + LIGHT[1] * grad_y[0] + LIGHT[2] * grad_x[0]
    slope_dens = grad_z[0] * grad_z[0] + grad_y[0] * grad_y[0] + grad_x[0] * grad_x[0]
    shading = 0.35 + 0.65 * facing * facing / (slope_dens + 0.05)
    slope_temp = grad_z[1] * grad_z[1] + grad_y[1] * grad_y[1] + grad_x[1] * grad_x[1]
    opacity_gain = 0.25 + 1.5 * slope_temp / (slope_temp + 0.1)
    entries = extinction.shape[0]
    position = (entries - 1) * jax.nn.sigmoid(2.0 * centre[0])
    tables = jnp.concatenate([extinction[None, :], colors.T], axis=0)
    looked = table_lookup(tables, position)
    optical = looked[0] * opacity_gain * step_len
    brighten = (1.0 + 0.5 * jnp.tanh(centre[2])) * jnp.exp(0.5 * jnp.tanh(centre[3])) * shading
    emission = looked[1:] * brighten
    return optical, emission


def composite(optical, emission):
    running = jnp.cumsum(optical, axis=0)
    weight = jnp.exp(optical - running) * (-jnp.expm1(-optical))
    color = jnp.sum(weight[None] * emission, axis=1)
    through = jnp.exp(-running[-1])
    return color, through


def reference(volume, extinction, palette, palette_index):
    colors = palette[palette_index]
    step_len = 0.25 / NZ

    def column_strip(column):
        first_col = column * CX
        middle = lax.dynamic_slice_in_dim(volume, first_col, CX, 3)
        margin_lo = lax.dynamic_slice_in_dim(volume, jnp.maximum(first_col - 3, 0).astype(jnp.int32), 3, 3)
        margin_hi = lax.dynamic_slice_in_dim(volume, jnp.minimum(first_col + CX, NX - 3).astype(jnp.int32), 3, 3)
        margin_lo = jnp.where(column > 0, margin_lo, 0.0)
        margin_hi = jnp.where(column < N_GX - 1, margin_hi, 0.0)
        widened = jnp.concatenate([margin_lo, middle, margin_hi], axis=3)
        smoothed = smooth_valid(smooth_zero(smooth_zero(widened, 1), 2), 3)
        x_cells = first_col - 1 + jnp.arange(CX + 2, dtype=jnp.int32)
        inside = ((x_cells >= 0) & (x_cells < NX)).astype(jnp.float32)
        smoothed = smoothed * inside
        fields = jnp.pad(smoothed[:2], ((0, 0), (1, 1), (0, 0), (0, 0)))
        centre = smoothed[:, :, :, 1:-1]
        optical, emission = emission_terms(centre, fields, extinction, colors, step_len)
        color, through = composite(optical, emission)
        return jnp.concatenate([color, 1.0 - through[None]], axis=0).reshape(4, HEIGHT * CX)

    strips = lax.map(column_strip, jnp.arange(N_GX, dtype=jnp.int32))
    return jnp.transpose(strips, (1, 0, 2))
```

```python
import functools

import jax
import jax.numpy as jnp
import ml_dtypes
import numpy as np
from jax import lax
from jax.experimental import pallas as pl
from jax.experimental.pallas import tpu as pltpu
from jax.sharding import PartitionSpec as P

TAPS = (0.0625, 0.25, 0.375, 0.25, 0.0625)
LIGHT = (0.64, 0.6, 0.48)
MESH = pl.DeviceIdType.MESH
F32 = jnp.float32
BF16 = jnp.bfloat16


def tap(distance):
    return TAPS[distance + 2] if -2 <= distance <= 2 else 0.0


def depth_height_weights(layers, height):
    along_z = np.array([[tap(z - (i - 2)) for z in range(layers)] for i in range(layers + 4)])
    along_y = np.array([[tap(yy - y) for yy in range(height)] for y in range(height)])
    return np.kron(along_z, along_y).astype(ml_dtypes.bfloat16)


def width_weights(width):
    result = np.zeros((3, 2, 2 * width, 2 * width))
    for kind in range(3):
        cells = np.arange(-3, width + 3)
        full = np.array([[tap(c - x) for x in range(-1, width + 1)] for c in cells])
        if kind == 0:
            full[:3] = 0.0
            full[:, 0] = 0.0
        if kind == 2:
            full[-3:] = 0.0
            full[:, -1] = 0.0
        both = np.concatenate([full[:, 1:-1], 0.5 * (full[:, 2:] - full[:, :-2])], axis=1)
        for slot in range(2):
            result[kind, slot, :width] = both[3:-3]
            result[kind, slot, width + 4 * slot : width + 4 * slot + 3] = both[:3]
            result[kind, slot, width + 8 + 4 * slot : width + 8 + 4 * slot + 3] = both[-3:]
    return result.astype(ml_dtypes.bfloat16)


def edge_selector(width):
    result = np.zeros((16, 2 * width))
    for slot in range(2):
        for c in range(3):
            result[4 * slot + c, slot * width + width - 3 + c] = 1.0
            result[8 + 4 * slot + c, slot * width + c] = 1.0
    return result.astype(ml_dtypes.bfloat16)


def halves(values):
    high = values.astype(BF16)
    return high, (values - high.astype(F32)).astype(BF16)


def dot(a, b, dims=((1,), (0,))):
    return lax.dot_general(a, b, (dims, ((), ())), preferred_element_type=F32)


def kernel(
    n_gx, n_depth, cells_z,
    vol_hbm, ext_hbm, pal_hbm, pidx_hbm, zy_hbm, xw_hbm, sel_hbm,
    out_ref,
    vol, ext, pal, pidx, zy, xw, sel, tab,
    part, edge_out, edge_in, corner_in, z01_in, z23_in,
    smooth, slope, piece_out, piece_in,
    load_sem, send_sem, recv_sem, piece_send, piece_recv,
):
    gx = lax.axis_index("gx")
    me = lax.axis_index("depth")
    left, right = lax.rem(gx + n_gx - 1, n_gx), lax.rem(gx + 1, n_gx)
    near, far = lax.rem(me + n_depth - 1, n_depth), lax.rem(me + 1, n_depth)
    layers, height, width = vol.shape[1], vol.shape[2], vol.shape[3]

    kind = jnp.where(gx == 0, 0, jnp.where(gx == n_gx - 1, 2, 1))
    loads = [
        pltpu.make_async_copy(vol_hbm, vol, load_sem.at[0]),
        pltpu.make_async_copy(zy_hbm, zy, load_sem.at[1]),
        pltpu.make_async_copy(sel_hbm, sel, load_sem.at[2]),
        pltpu.make_async_copy(xw_hbm.at[kind], xw, load_sem.at[3]),
        pltpu.make_async_copy(ext_hbm, ext, load_sem.at[4]),
        pltpu.make_async_copy(pal_hbm, pal, load_sem.at[5]),
        pltpu.make_async_copy(pidx_hbm, pidx, load_sem.at[6]),
    ]
    for load in loads:
        load.start()

    barrier = pltpu.get_barrier_semaphore()
    for gx_to in (left, right):
        for depth_to in (near, me, far):
            pl.semaphore_signal(barrier, inc=1, device_id=(gx_to, depth_to), device_id_type=MESH)

    @pl.loop(1, n_depth)
    def _(step):
        to = lax.rem(me + step, n_depth)
        pl.semaphore_signal(barrier, inc=1, device_id=(gx, to), device_id_type=MESH)

    for load in loads[:3]:
        load.wait()

    for pair in range(2):
        raw = jnp.concatenate(
            [vol[2 * pair + f].reshape(layers * height, width) for f in range(2)], axis=1
        )
        high, low = halves(raw)
        spread = dot(zy[...], high) + dot(zy[...], low)
        for f in range(2):
            part[2 * pair + f] = spread[:, f * width : (f + 1) * width].reshape(
                layers + 4, height, width
            )
        high, low = halves(spread)
        edges = dot(sel[...], high, ((1,), (1,))) + dot(sel[...], low, ((1,), (1,)))
        for side in range(2):
            for k in range(3):
                edge_out[side, k, pair] = edges[
                    8 * side : 8 * side + 8, 128 * k : 128 * k + 128
                ]

    pl.semaphore_wait(barrier, n_depth + 5)

    def send(number, source, target, gx_to, depth_to):
        copy = pltpu.make_async_remote_copy(
            src_ref=source,
            dst_ref=target,
            send_sem=send_sem.at[number],
            recv_sem=recv_sem.at[number],
            device_id=(gx_to, depth_to),
            device_id_type=MESH,
        )
        copy.start()
        return copy

    copies = [
        send(0, part.at[pl.ds(0, 2), pl.ds(layers + 1, 3)], z01_in.at[0], gx, far),
        send(1, part.at[pl.ds(0, 2), pl.ds(0, 3)], z01_in.at[1], gx, near),
        send(2, part.at[pl.ds(2, 2), pl.ds(layers + 2, 2)], z23_in.at[0], gx, far),
        send(3, part.at[pl.ds(2, 2), pl.ds(0, 2)], z23_in.at[1], gx, near),
        send(4, edge_out.at[0, 2], corner_in.at[0, 0], right, far),
        send(5, edge_out.at[1, 2], corner_in.at[0, 1], left, far),
        send(6, edge_out.at[0, 0], corner_in.at[1, 0], right, near),
        send(7, edge_out.at[1, 0], corner_in.at[1, 1], left, near),
        send(8, edge_out.at[0], edge_in.at[0], right, me),
        send(9, edge_out.at[1], edge_in.at[1], left, me),
    ]

    for load in loads[3:]:
        load.wait()

    step_len = 0.25 / cells_z
    rows = lax.broadcasted_iota(jnp.int32, (pal.shape[0], 128), 0)
    chosen = pidx[...] == rows
    entries = [ext[...] * step_len] + [
        jnp.sum(jnp.where(chosen, pal[:, c : c + 1], 0.0), axis=0, keepdims=True)
        for c in range(3)
    ]
    table = jnp.concatenate(entries, axis=0)
    tab[0:4] = table
    tab[4:8] = jnp.concatenate([table[:, 1:], table[:, :1]], axis=1) - table

    zeros8 = jnp.zeros((layers + 4, 8, width), F32)
    for f in range(2):
        smooth[f, :, 0:8] = zeros8
        smooth[f, :, height + 8 : height + 16] = zeros8

    for copy in copies:
        copy.wait_recv()

    has_near = jnp.where(me > 0, 1.0, 0.0).astype(F32)
    has_far = jnp.where(me < n_depth - 1, 1.0, 0.0).astype(F32)
    for k in range(3):
        for pair in range(2):
            edge = jnp.concatenate([edge_in[0, k, pair], edge_in[1, k, pair]], axis=0)
            if k == 0:
                edge += has_near * jnp.concatenate(
                    [corner_in[0, 0, pair], corner_in[0, 1, pair]], axis=0
                )
            if k == 2:
                edge += has_far * jnp.concatenate(
                    [corner_in[1, 0, pair], corner_in[1, 1, pair]], axis=0
                )
            edge = jnp.concatenate([edge, jnp.zeros((112, 128), F32)], axis=0)
            edge = jnp.transpose(edge)
            for f in range(2):
                field = 2 * pair + f
                body = [part[field, 4 * k + j] for j in range(4)]
                if pair == 0 and k == 0:
                    body = [body[0]] + [body[1 + j] + has_near * z01_in[0, f, j] for j in range(3)]
                if pair == 0 and k == 2:
                    body = [body[j] + has_far * z01_in[1, f, j] for j in range(3)] + [body[3]]
                if pair == 1 and k == 0:
                    body = body[:2] + [body[2 + j] + has_near * z23_in[0, f, j] for j in range(2)]
                if pair == 1 and k == 2:
                    body = [body[j] + has_far * z23_in[1, f, j] for j in range(2)] + body[2:]
                rows = jnp.concatenate(body, axis=0)
                high, low = halves(jnp.concatenate([rows, edge], axis=1))
                if pair == 0:
                    weights = xw[f]
                    found = dot(high, weights) + dot(low, weights)
                    here = found[:, :width].reshape(4, height, width)
                    for j in range(4):
                        layer = here[j]
                        if 4 * k + j == 1:
                            layer = layer * has_near
                        if 4 * k + j == layers + 2:
                            layer = layer * has_far
                        smooth[field, 4 * k + j, 8 : height + 8] = layer
                    slope[f, 4 * k : 4 * k + 4] = found[:, width:].reshape(4, height, width)
                else:
                    weights = xw[f, :, :width]
                    found = dot(high, weights) + dot(low, weights)
                    smooth[field, 4 * k : 4 * k + 4, 8 : height + 8] = found.reshape(
                        4, height, width
                    )

    top = ext.shape[1] - 1

    def look(row, at, fraction):
        def pick(r):
            entry = jnp.broadcast_to(tab[r : r + 1], (layers * 8, 128))
            return jnp.take_along_axis(entry, at, axis=1, mode="promise_in_bounds")

        return (pick(row) + fraction * pick(row + 4)).reshape(layers, 8, width)

    for t in range(height // 8):
        here = pl.ds(8 * t + 8, 8)
        grads = []
        for f in range(2):
            grads.append(
                (
                    0.5 * (smooth[f, 3 : layers + 3, here] - smooth[f, 1 : layers + 1, here]),
                    0.5
                    * (
                        smooth[f, 2 : layers + 2, 8 * t + 9 : 8 * t + 17]
                        - smooth[f, 2 : layers + 2, 8 * t + 7 : 8 * t + 15]
                    ),
                    slope[f, 2 : layers + 2, pl.ds(8 * t, 8)],
                )
            )
        z0, y0, x0 = grads[0]
        z1, y1, x1 = grads[1]
        facing = LIGHT[0] * z0 + LIGHT[1] * y0 + LIGHT[2] * x0
        steep = z0 * z0 + y0 * y0 + x0 * x0
        shading = 0.35 + 0.65 * facing * facing / (steep + 0.05)
        warm = z1 * z1 + y1 * y1 + x1 * x1
        gain = 0.25 + 1.5 * warm / (warm + 0.1)
        place = (0.5 * top) * (1.0 + jnp.tanh(smooth[0, 2 : layers + 2, here]))
        at = jnp.clip(place.astype(jnp.int32), 0, top - 1)
        fraction = (place - at.astype(F32)).reshape(layers * 8, width)
        at = at.reshape(layers * 8, width)
        tau = look(0, at, fraction) * gain
        bright = (
            (1.0 + 0.5 * jnp.tanh(smooth[2, 2 : layers + 2, here]))
            * jnp.exp(0.5 * jnp.tanh(smooth[3, 2 : layers + 2, here]))
            * shading
        )
        absorbed = tau * (
            1.0
            - tau * (1 / 2)
            * (1.0 - tau * (1 / 3) * (1.0 - tau * (1 / 4) * (1.0 - tau * (1 / 5) * (1.0 - tau * (1 / 6)))))
        )
        opaque = jnp.zeros((8, width), F32)
        weights = []
        for z in range(layers):
            weight = absorbed[z] - absorbed[z] * opaque
            weights.append(weight[None])
            opaque = opaque + weight
        weight = jnp.concatenate(weights, axis=0) * bright
        for c in range(3):
            piece_out[pl.ds(8 * t, 8), c] = jnp.sum(weight * look(1 + c, at, fraction), axis=0)
        piece_out[pl.ds(8 * t, 8), 3] = opaque

    def piece(to):
        return pltpu.make_async_remote_copy(
            src_ref=piece_out.at[to],
            dst_ref=piece_in.at[me],
            send_sem=piece_send,
            recv_sem=piece_recv,
            device_id=(gx, to),
            device_id_type=MESH,
        )

    @pl.loop(1, n_depth)
    def _(step):
        piece(lax.rem(me + step, n_depth)).start()

    own = pltpu.make_async_copy(piece_out.at[me], piece_in.at[me], piece_recv)
    own.start()
    for copy in copies:
        copy.wait_send()
    pltpu.make_async_copy(piece_in, piece_in, piece_recv).wait()
    others = piece_out.at[pl.ds(0, n_depth - 1)]
    pltpu.make_async_copy(others, others, piece_send).wait()

    group = n_depth // 8

    def over(nearer, farther):
        through = 1.0 - nearer[3]
        return [nearer[c] + through * farther[c] for c in range(4)]

    pieces = [
        [jnp.concatenate([piece_in[s * group + j, c : c + 1] for s in range(8)], axis=0) for c in range(4)]
        for j in range(group)
    ]
    total = pieces[0]
    for j in range(1, group):
        total = over(total, pieces[j])
    size = 8
    while size > 1:
        size //= 2
        nearer = [jnp.concatenate([v[2 * i : 2 * i + 1] for i in range(size)], axis=0) for v in total]
        farther = [jnp.concatenate([v[2 * i + 1 : 2 * i + 2] for i in range(size)], axis=0) for v in total]
        total = over(nearer, farther)
    out_ref[...] = jnp.concatenate(total, axis=0)


def solution(mesh):
    n_gx, n_depth = mesh.shape["gx"], mesh.shape["depth"]

    def per_device(volume, extinction, palette, palette_index):
        fields, layers, height, width = volume.shape
        entries = extinction.shape[0]
        colours = palette.shape[0]
        zy = depth_height_weights(layers, height)
        xw = width_weights(width)
        sel = edge_selector(width)
        anywhere = pl.BlockSpec(memory_space=pl.ANY)
        image = pl.pallas_call(
            functools.partial(kernel, n_gx, n_depth, layers * n_depth),
            out_shape=jax.ShapeDtypeStruct((4, width), F32),
            in_specs=[anywhere] * 7,
            out_specs=pl.BlockSpec(memory_space=pltpu.VMEM),
            scratch_shapes=[
                pltpu.VMEM(volume.shape, F32),
                pltpu.VMEM((1, entries), F32),
                pltpu.VMEM((colours, 3), F32),
                pltpu.VMEM((1, entries), jnp.int32),
                pltpu.VMEM(zy.shape, BF16),
                pltpu.VMEM(xw.shape[1:], BF16),
                pltpu.VMEM(sel.shape, BF16),
                pltpu.VMEM((8, entries), F32),
                pltpu.VMEM((fields, layers + 4, height, width), F32),
                pltpu.VMEM((2, 3, 2, 8, 128), F32),
                pltpu.VMEM((2, 3, 2, 8, 128), F32),
                pltpu.VMEM((2, 2, 2, 8, 128), F32),
                pltpu.VMEM((2, 2, 3, height, width), F32),
                pltpu.VMEM((2, 2, 2, height, width), F32),
                pltpu.VMEM((fields, layers + 4, height + 16, width), F32),
                pltpu.VMEM((2, layers + 4, height, width), F32),
                pltpu.VMEM((n_depth, 4, width), F32),
                pltpu.VMEM((n_depth, 4, width), F32),
                pltpu.SemaphoreType.DMA((7,)),
                pltpu.SemaphoreType.DMA((10,)),
                pltpu.SemaphoreType.DMA((10,)),
                pltpu.SemaphoreType.DMA,
                pltpu.SemaphoreType.DMA,
            ],
            compiler_params=pltpu.CompilerParams(
                collective_id=0, has_side_effects=True, vmem_limit_bytes=32 * 1024 * 1024
            ),
        )(
            volume,
            extinction.reshape(1, entries),
            palette,
            palette_index.reshape(1, entries),
            jnp.asarray(zy),
            jnp.asarray(xw),
            jnp.asarray(sel),
        )
        return image.reshape(4, 1, width)

    placed = (P(None, "depth", None, "gx"), P(), P(), P())
    return jax.shard_map(
        per_device, mesh=mesh, in_specs=placed, out_specs=P(None, "gx", "depth"), check_vma=False
    )
```

```python
import functools

import jax
import jax.numpy as jnp
import ml_dtypes
import numpy as np
from jax import lax
from jax.experimental import pallas as pl
from jax.experimental.pallas import tpu as pltpu
from jax.sharding import PartitionSpec as P

TAPS = (0.0625, 0.25, 0.375, 0.25, 0.0625)
LIGHT = (0.64, 0.6, 0.48)
MESH = pl.DeviceIdType.MESH
SEND_ORDER = (4, 5, 6, 7, 8, 9, 0, 1, 2, 3)
VMEM_BYTES = 63 * 1024 * 1024
F32 = jnp.float32
BF16 = jnp.bfloat16


def tap(distance):
    return TAPS[distance + 2] if -2 <= distance <= 2 else 0.0


def depth_height_weights(layers, height):
    along_z = np.array([[tap(z - (i - 2)) for z in range(layers)] for i in range(layers + 4)])
    along_y = np.array([[tap(yy - y) for yy in range(height)] for y in range(height)])
    return np.kron(along_z, along_y).astype(ml_dtypes.bfloat16)


def width_weights(width):
    result = np.zeros((3, 2, 2 * width, 2 * width))
    for kind in range(3):
        cells = np.arange(-3, width + 3)
        full = np.array([[tap(c - x) for x in range(-1, width + 1)] for c in cells])
        if kind == 0:
            full[:3] = 0.0
            full[:, 0] = 0.0
        if kind == 2:
            full[-3:] = 0.0
            full[:, -1] = 0.0
        both = np.concatenate([full[:, 1:-1], 0.5 * (full[:, 2:] - full[:, :-2])], axis=1)
        for slot in range(2):
            result[kind, slot, :width] = both[3:-3]
            result[kind, slot, width + 4 * slot : width + 4 * slot + 3] = both[:3]
            result[kind, slot, width + 8 + 4 * slot : width + 8 + 4 * slot + 3] = both[-3:]
    return result.astype(ml_dtypes.bfloat16)


def edge_selector(width):
    result = np.zeros((16, 2 * width))
    for slot in range(2):
        for c in range(3):
            result[4 * slot + c, slot * width + width - 3 + c] = 1.0
            result[8 + 4 * slot + c, slot * width + c] = 1.0
    return result.astype(ml_dtypes.bfloat16)


def halves(values):
    high = values.astype(BF16)
    return high, (values - high.astype(F32)).astype(BF16)


def dot(a, b, dims=((1,), (0,))):
    return lax.dot_general(a, b, (dims, ((), ())), preferred_element_type=F32)


def kernel(
    n_gx, n_depth, cells_z,
    vol_hbm, ext_hbm, pal_hbm, pidx_hbm, zy_hbm, xw_hbm, sel_hbm,
    out_ref,
    vol, ext, pal, pidx, zy, xw, sel, tab,
    part, edge_out, edge_in, corner_in, z01_in, z23_in,
    smooth, slope, piece_out, piece_in,
    load_sem, send_sem, recv_sem, piece_send, piece_recv, known_sem,
):
    gx = lax.axis_index("gx")
    me = lax.axis_index("depth")
    layers, height, width = vol.shape[1], vol.shape[2], vol.shape[3]
    has_left, has_right = gx > 0, gx < n_gx - 1
    has_near, has_far = me > 0, me < n_depth - 1

    first = pltpu.make_async_copy(vol_hbm, vol, load_sem.at[0])
    first.start()

    barrier = pltpu.get_barrier_semaphore()

    def around(distance):
        return lax.rem(me + n_depth + distance, n_depth)

    def greet(gx_to, depth_to, there):
        @pl.when(there)
        def _():
            pl.semaphore_signal(barrier, inc=1, device_id=(gx_to, depth_to), device_id_type=MESH)

    for step, there in ((-1, has_near), (1, has_far), (0, True)):
        greet(gx - 1, me + step, has_left & there)
        greet(gx + 1, me + step, has_right & there)
    reach = 4
    for distance in range(1, reach + 1):
        for depth_to in (around(distance), around(-distance)):
            pl.semaphore_signal(barrier, inc=1, device_id=(gx, depth_to), device_id_type=MESH)

    kind = jnp.where(has_left, jnp.where(has_right, 1, 2), 0)
    loads = [
        pltpu.make_async_copy(zy_hbm, zy, load_sem.at[1]),
        pltpu.make_async_copy(sel_hbm, sel, load_sem.at[2]),
        pltpu.make_async_copy(xw_hbm.at[kind], xw, load_sem.at[3]),
        pltpu.make_async_copy(ext_hbm, ext, load_sem.at[4]),
        pltpu.make_async_copy(pal_hbm, pal, load_sem.at[5]),
        pltpu.make_async_copy(pidx_hbm, pidx, load_sem.at[6]),
    ]
    for load in loads:
        load.start()
    loads = [first] + loads
    for load in loads[:3]:
        load.wait()

    for pair in range(2):
        raw = jnp.concatenate(
            [vol[2 * pair + f].reshape(layers * height, width) for f in range(2)], axis=1
        )
        high, low = halves(raw)
        spread = dot(zy[...], high) + dot(zy[...], low)
        for f in range(2):
            part[2 * pair + f] = spread[:, f * width : (f + 1) * width].reshape(
                layers + 4, height, width
            )
        high, low = halves(spread)
        edges = dot(sel[...], high, ((1,), (1,))) + dot(sel[...], low, ((1,), (1,)))
        for side in range(2):
            for k in range(3):
                edge_out[side, k, pair] = edges[
                    8 * side : 8 * side + 8, 128 * k : 128 * k + 128
                ]

    n_sides = has_left.astype(jnp.int32) + has_right.astype(jnp.int32)
    n_rows = 1 + has_near.astype(jnp.int32) + has_far.astype(jnp.int32)
    pl.semaphore_wait(barrier, 2 * reach + n_sides * n_rows)

    near2, far2 = pl.ds(0, 2), pl.ds(2, 2)
    table = [
        (part.at[near2, pl.ds(layers + 1, 3)], z01_in.at[0], gx, me + 1, has_far, has_near),
        (part.at[near2, pl.ds(0, 3)], z01_in.at[1], gx, me - 1, has_near, has_far),
        (part.at[far2, pl.ds(layers + 2, 2)], z23_in.at[0], gx, me + 1, has_far, has_near),
        (part.at[far2, pl.ds(0, 2)], z23_in.at[1], gx, me - 1, has_near, has_far),
        (edge_out.at[0, 2], corner_in.at[0, 0], gx + 1, me + 1, has_right & has_far, has_left & has_near),
        (edge_out.at[1, 2], corner_in.at[0, 1], gx - 1, me + 1, has_left & has_far, has_right & has_near),
        (edge_out.at[0, 0], corner_in.at[1, 0], gx + 1, me - 1, has_right & has_near, has_left & has_far),
        (edge_out.at[1, 0], corner_in.at[1, 1], gx - 1, me - 1, has_left & has_near, has_right & has_far),
        (edge_out.at[0], edge_in.at[0], gx + 1, me, has_right, has_left),
        (edge_out.at[1], edge_in.at[1], gx - 1, me, has_left, has_right),
    ]

    def copy(number):
        source, target, gx_to, depth_to = table[number][:4]
        return pltpu.make_async_remote_copy(
            src_ref=source,
            dst_ref=target,
            send_sem=send_sem.at[number],
            recv_sem=recv_sem.at[number],
            device_id=(gx_to, depth_to),
            device_id_type=MESH,
        )

    for number in SEND_ORDER:
        @pl.when(table[number][4])
        def _():
            copy(number).start()

    def know():
        for depth_to in (around(reach), around(-reach)):
            pl.semaphore_signal(
                known_sem.at[reach.bit_length() - 3], inc=1, device_id=(gx, depth_to), device_id_type=MESH
            )

    know()
    for _, target, _, _, _, comes in table:
        @pl.when(jnp.logical_not(comes))
        def _():
            target[...] = jnp.zeros(target.shape, F32)

    for load in loads[3:]:
        load.wait()

    step_len = 0.25 / cells_z
    colours = pal.shape[1]
    spread = jnp.concatenate([pal[...], jnp.zeros((3, 128 - colours), F32)], axis=1)
    chosen = jnp.broadcast_to(pidx[...], (8, 128))
    entries = [ext[...] * step_len] + [
        jnp.take_along_axis(
            jnp.broadcast_to(spread[c : c + 1], (8, 128)), chosen, axis=1, mode="promise_in_bounds"
        )[0:1]
        for c in range(3)
    ]
    entries = jnp.concatenate(entries, axis=0)
    tab[0:4] = entries
    tab[4:8] = jnp.concatenate([entries[:, 1:], entries[:, :1]], axis=1) - entries

    zeros8 = jnp.zeros((layers + 4, 8, width), F32)
    for f in range(2):
        smooth[f, :, 0:8] = zeros8
        smooth[f, :, height + 8 : height + 16] = zeros8

    while 2 * reach < n_depth // 2:
        pl.semaphore_wait(known_sem.at[reach.bit_length() - 3], 2)
        reach *= 2
        know()

    def arrived(*numbers):
        for number in numbers:
            @pl.when(table[number][5])
            def _():
                copy(number).wait_recv()

    keep_near = jnp.where(has_near, 1.0, 0.0).astype(F32)
    keep_far = jnp.where(has_far, 1.0, 0.0).astype(F32)

    def filter_width(k, pair):
        edge = jnp.concatenate([edge_in[0, k, pair], edge_in[1, k, pair]], axis=0)
        if k != 1:
            edge += jnp.concatenate(
                [corner_in[k // 2, 0, pair], corner_in[k // 2, 1, pair]], axis=0
            )
        edge = jnp.transpose(jnp.concatenate([edge, jnp.zeros((112, 128), F32)], axis=0))
        for f in range(2):
            field = 2 * pair + f
            body = [part[field, 4 * k + j] for j in range(4)]
            came, count = (z01_in, 3) if pair == 0 else (z23_in, 2)
            if k == 0:
                for j in range(count):
                    body[4 - count + j] += came[0, f, j]
            if k == 2:
                for j in range(count):
                    body[j] += came[1, f, j]
            rows = jnp.concatenate(body, axis=0)
            high, low = halves(jnp.concatenate([rows, edge], axis=1))
            if pair == 0:
                weights = xw[f]
                found = dot(high, weights) + dot(low, weights)
                here = found[:, :width].reshape(4, height, width)
                for j in range(4):
                    layer = here[j]
                    if 4 * k + j == 1:
                        layer = layer * keep_near
                    if 4 * k + j == layers + 2:
                        layer = layer * keep_far
                    smooth[field, 4 * k + j, 8 : height + 8] = layer
                slope[f, 4 * k : 4 * k + 4] = found[:, width:].reshape(4, height, width)
            else:
                weights = xw[f, :, :width]
                found = dot(high, weights) + dot(low, weights)
                smooth[field, 4 * k : 4 * k + 4, 8 : height + 8] = found.reshape(
                    4, height, width
                )

    arrived(8, 9)
    filter_width(1, 0)
    filter_width(1, 1)
    arrived(4, 5, 6, 7, 0, 1)
    filter_width(0, 0)
    filter_width(2, 0)
    arrived(2, 3)
    filter_width(0, 1)
    filter_width(2, 1)

    top = ext.shape[1] - 1

    def look(row, at, fraction):
        def pick(r):
            entry = jnp.broadcast_to(tab[r : r + 1], (layers * 8, 128))
            return jnp.take_along_axis(entry, at, axis=1, mode="promise_in_bounds")

        return (pick(row) + fraction * pick(row + 4)).reshape(layers, 8, width)

    def piece(to):
        return pltpu.make_async_remote_copy(
            src_ref=piece_out.at[to],
            dst_ref=piece_in.at[me],
            send_sem=piece_send,
            recv_sem=piece_recv,
            device_id=(gx, to),
            device_id_type=MESH,
        )

    for t in range(height // 8):
        here = pl.ds(8 * t + 8, 8)
        grads = []
        for f in range(2):
            grads.append(
                (
                    0.5 * (smooth[f, 3 : layers + 3, here] - smooth[f, 1 : layers + 1, here]),
                    0.5
                    * (
                        smooth[f, 2 : layers + 2, 8 * t + 9 : 8 * t + 17]
                        - smooth[f, 2 : layers + 2, 8 * t + 7 : 8 * t + 15]
                    ),
                    slope[f, 2 : layers + 2, pl.ds(8 * t, 8)],
                )
            )
        z0, y0, x0 = grads[0]
        z1, y1, x1 = grads[1]
        facing = LIGHT[0] * z0 + LIGHT[1] * y0 + LIGHT[2] * x0
        steep = z0 * z0 + y0 * y0 + x0 * x0
        shading = 0.35 + 0.65 * facing * facing / (steep + 0.05)
        warm = z1 * z1 + y1 * y1 + x1 * x1
        gain = 0.25 + 1.5 * warm / (warm + 0.1)
        place = (0.5 * top) * (1.0 + jnp.tanh(smooth[0, 2 : layers + 2, here]))
        at = jnp.clip(place.astype(jnp.int32), 0, top - 1)
        fraction = (place - at.astype(F32)).reshape(layers * 8, width)
        at = at.reshape(layers * 8, width)
        tau = look(0, at, fraction) * gain
        bright = (
            (1.0 + 0.5 * jnp.tanh(smooth[2, 2 : layers + 2, here]))
            * jnp.exp(0.5 * jnp.tanh(smooth[3, 2 : layers + 2, here]))
            * shading
        )
        absorbed = tau * (
            1.0
            - tau * (1 / 2)
            * (1.0 - tau * (1 / 3) * (1.0 - tau * (1 / 4) * (1.0 - tau * (1 / 5) * (1.0 - tau * (1 / 6)))))
        )
        opaque = jnp.zeros((8, width), F32)
        weights = []
        for z in range(layers):
            weight = absorbed[z] - absorbed[z] * opaque
            weights.append(weight[None])
            opaque = opaque + weight
        weight = jnp.concatenate(weights, axis=0) * bright
        for c in range(3):
            piece_out[pl.ds(8 * t, 8), c] = jnp.sum(weight * look(1 + c, at, fraction), axis=0)
        piece_out[pl.ds(8 * t, 8), 3] = opaque
        if t == 0:
            pl.semaphore_wait(known_sem.at[reach.bit_length() - 3], 2)

        @pl.loop(8 * t, 8 * t + 8)
        def _(to):
            @pl.when(to != me)
            def _():
                piece(to).start()

    own = pltpu.make_async_copy(piece_out.at[me], piece_in.at[me], piece_recv)
    own.start()
    for number in range(len(table)):
        @pl.when(table[number][4])
        def _():
            copy(number).wait_send()
    pltpu.make_async_copy(piece_in, piece_in, piece_recv).wait()
    others = piece_out.at[pl.ds(0, n_depth - 1)]
    pltpu.make_async_copy(others, others, piece_send).wait()

    group = n_depth // 8

    def over(nearer, farther):
        through = 1.0 - nearer[3]
        return [nearer[c] + through * farther[c] for c in range(4)]

    pieces = [
        [jnp.concatenate([piece_in[s * group + j, c : c + 1] for s in range(8)], axis=0) for c in range(4)]
        for j in range(group)
    ]
    total = pieces[0]
    for j in range(1, group):
        total = over(total, pieces[j])
    size = 8
    while size > 1:
        size //= 2
        nearer = [jnp.concatenate([v[2 * i : 2 * i + 1] for i in range(size)], axis=0) for v in total]
        farther = [jnp.concatenate([v[2 * i + 1 : 2 * i + 2] for i in range(size)], axis=0) for v in total]
        total = over(nearer, farther)
    out_ref[...] = jnp.concatenate(total, axis=0)


def solution(mesh):
    n_gx, n_depth = mesh.shape["gx"], mesh.shape["depth"]

    def per_device(volume, extinction, palette, palette_index):
        fields, layers, height, width = volume.shape
        entries = extinction.shape[0]
        colours = palette.shape[0]
        zy = depth_height_weights(layers, height)
        xw = width_weights(width)
        sel = edge_selector(width)
        anywhere = pl.BlockSpec(memory_space=pl.ANY)
        image = pl.pallas_call(
            functools.partial(kernel, n_gx, n_depth, layers * n_depth),
            out_shape=jax.ShapeDtypeStruct((4, width), F32),
            in_specs=[anywhere] * 7,
            out_specs=pl.BlockSpec(memory_space=pltpu.VMEM),
            scratch_shapes=[
                pltpu.VMEM(volume.shape, F32),
                pltpu.VMEM((1, entries), F32),
                pltpu.VMEM((3, colours), F32),
                pltpu.VMEM((1, entries), jnp.int32),
                pltpu.VMEM(zy.shape, BF16),
                pltpu.VMEM(xw.shape[1:], BF16),
                pltpu.VMEM(sel.shape, BF16),
                pltpu.VMEM((8, entries), F32),
                pltpu.VMEM((fields, layers + 4, height, width), F32),
                pltpu.VMEM((2, 3, 2, 8, 128), F32),
                pltpu.VMEM((2, 3, 2, 8, 128), F32),
                pltpu.VMEM((2, 2, 2, 8, 128), F32),
                pltpu.VMEM((2, 2, 3, height, width), F32),
                pltpu.VMEM((2, 2, 2, height, width), F32),
                pltpu.VMEM((fields, layers + 4, height + 16, width), F32),
                pltpu.VMEM((2, layers + 4, height, width), F32),
                pltpu.VMEM((n_depth, 4, width), F32),
                pltpu.VMEM((n_depth, 4, width), F32),
                pltpu.SemaphoreType.DMA((7,)),
                pltpu.SemaphoreType.DMA((10,)),
                pltpu.SemaphoreType.DMA((10,)),
                pltpu.SemaphoreType.DMA,
                pltpu.SemaphoreType.DMA,
                pltpu.SemaphoreType.REGULAR((2,)),
            ],
            compiler_params=pltpu.CompilerParams(
                collective_id=0, has_side_effects=True, vmem_limit_bytes=VMEM_BYTES
            ),
        )(
            volume,
            extinction.reshape(1, entries),
            palette.T,
            palette_index.reshape(1, entries),
            jnp.asarray(zy),
            jnp.asarray(xw),
            jnp.asarray(sel),
        )
        return image.reshape(4, 1, width)

    placed = (P(None, "depth", None, "gx"), P(), P(), P())
    return jax.shard_map(
        per_device, mesh=mesh, in_specs=placed, out_specs=P(None, "gx", "depth"), check_vma=False
    )
```

```python
import functools

import jax
import jax.numpy as jnp
import ml_dtypes
import numpy as np
from jax import lax
from jax.experimental import pallas as pl
from jax.experimental.pallas import tpu as pltpu
from jax.sharding import PartitionSpec as P

TAPS = (0.0625, 0.25, 0.375, 0.25, 0.0625)
LIGHT = (0.64, 0.6, 0.48)
MESH = pl.DeviceIdType.MESH
FIRST = 8
VMEM_BYTES = 63 * 1024 * 1024
F32 = jnp.float32
BF16 = jnp.bfloat16


def tap(distance):
    return TAPS[distance + 2] if -2 <= distance <= 2 else 0.0


def depth_height_weights(layers, height):
    along_z = np.array([[tap(z - (i - 2)) for z in range(layers)] for i in range(layers + 4)])
    along_y = np.array([[tap(yy - y) for yy in range(height)] for y in range(height)])
    return np.kron(along_z, along_y).astype(ml_dtypes.bfloat16)


def width_weights(width):
    result = np.zeros((3, 2, 2 * width, 2 * width))
    for kind in range(3):
        cells = np.arange(-3, width + 3)
        full = np.array([[tap(c - x) for x in range(-1, width + 1)] for c in cells])
        if kind == 0:
            full[:3] = 0.0
            full[:, 0] = 0.0
        if kind == 2:
            full[-3:] = 0.0
            full[:, -1] = 0.0
        both = np.concatenate([full[:, 1:-1], 0.5 * (full[:, 2:] - full[:, :-2])], axis=1)
        for slot in range(2):
            result[kind, slot, :width] = both[3:-3]
            result[kind, slot, width + 4 * slot : width + 4 * slot + 3] = both[:3]
            result[kind, slot, width + 8 + 4 * slot : width + 8 + 4 * slot + 3] = both[-3:]
    return result.astype(ml_dtypes.bfloat16)


def edge_selector(width):
    result = np.zeros((16, 2 * width))
    for slot in range(2):
        for c in range(3):
            result[4 * slot + c, slot * width + width - 3 + c] = 1.0
            result[8 + 4 * slot + c, slot * width + c] = 1.0
    return result.astype(ml_dtypes.bfloat16)


def halves(values):
    high = values.astype(BF16)
    return high, (values - high.astype(F32)).astype(BF16)


def dot(a, b, dims=((1,), (0,))):
    return lax.dot_general(a, b, (dims, ((), ())), preferred_element_type=F32)


def kernel(
    n_gx, n_depth, cells_z,
    vol_hbm, ext_hbm, pal_hbm, pidx_hbm, zy_hbm, xw_hbm, sel_hbm,
    out_ref,
    vol, ext, pal, pidx, zy, xw, sel, tab,
    part, edge_out, edge_in, corner_in, z01_in, z23_in,
    beside, smooth, slope, piece_out, piece_in,
    load_sem, send_sem, recv_sem, piece_send, piece_recv, known_sem,
):
    gx = lax.axis_index("gx")
    me = lax.axis_index("depth")
    layers, height, width = vol.shape[1], vol.shape[2], vol.shape[3]
    has_left, has_right = gx > 0, gx < n_gx - 1
    has_near, has_far = me > 0, me < n_depth - 1

    kind = jnp.where(has_left, jnp.where(has_right, 1, 2), 0)
    loads = [
        pltpu.make_async_copy(vol_hbm.at[pl.ds(0, 2)], vol.at[pl.ds(0, 2)], load_sem.at[0]),
        pltpu.make_async_copy(zy_hbm, zy, load_sem.at[1]),
        pltpu.make_async_copy(vol_hbm.at[pl.ds(2, 2)], vol.at[pl.ds(2, 2)], load_sem.at[2]),
        pltpu.make_async_copy(sel_hbm, sel, load_sem.at[3]),
        pltpu.make_async_copy(xw_hbm.at[kind], xw, load_sem.at[4]),
        pltpu.make_async_copy(ext_hbm, ext, load_sem.at[5]),
        pltpu.make_async_copy(pal_hbm, pal, load_sem.at[6]),
        pltpu.make_async_copy(pidx_hbm, pidx, load_sem.at[7]),
    ]
    for load in loads[:2]:
        load.start()

    barrier = pltpu.get_barrier_semaphore()

    def around(distance):
        return lax.rem(me + n_depth + distance, n_depth)

    def greet(gx_to, depth_to, there):
        @pl.when(there)
        def _():
            pl.semaphore_signal(barrier, inc=1, device_id=(gx_to, depth_to), device_id_type=MESH)

    for step, there in ((-1, has_near), (1, has_far), (0, True)):
        greet(gx - 1, me + step, has_left & there)
        greet(gx + 1, me + step, has_right & there)
    reach = 4
    for distance in range(reach, 0, -1):
        for depth_to in (around(distance), around(-distance)):
            pl.semaphore_signal(barrier, inc=1, device_id=(gx, depth_to), device_id_type=MESH)
    for load in loads[2:]:
        load.start()

    @pl.when(me < FIRST)
    def _():
        @pl.loop(reach + 1, n_depth - reach)
        def _(distance):
            pl.semaphore_signal(
                barrier, inc=1, device_id=(gx, around(distance)), device_id_type=MESH
            )

    n_first = 0
    for device in range(FIRST):
        apart = lax.rem(me + n_depth - device, n_depth)
        n_first += ((apart > reach) & (apart < n_depth - reach)).astype(jnp.int32)

    def know():
        for depth_to in (around(reach), around(-reach)):
            pl.semaphore_signal(
                known_sem.at[reach.bit_length() - 3], inc=1, device_id=(gx, depth_to), device_id_type=MESH
            )

    def filter_own(pair):
        raw = jnp.concatenate(
            [vol[2 * pair + f].reshape(layers * height, width) for f in range(2)], axis=1
        )
        high, low = halves(raw)
        spread = dot(zy[...], high) + dot(zy[...], low)
        for f in range(2):
            part[2 * pair + f] = spread[:, f * width : (f + 1) * width].reshape(
                layers + 4, height, width
            )
        high, low = halves(spread)
        edges = dot(sel[...], high, ((1,), (1,))) + dot(sel[...], low, ((1,), (1,)))
        for side in range(2):
            for k in range(3):
                edge_out[side, k, pair] = edges[
                    8 * side : 8 * side + 8, 128 * k : 128 * k + 128
                ]

    for load in (loads[0], loads[1], loads[3]):
        load.wait()
    filter_own(0)
    loads[2].wait()
    filter_own(1)
    n_sides = has_left.astype(jnp.int32) + has_right.astype(jnp.int32)
    n_rows = 1 + has_near.astype(jnp.int32) + has_far.astype(jnp.int32)
    pl.semaphore_wait(barrier, 2 * reach + n_sides * n_rows + n_first)
    know()

    table = [
        (edge_out.at[0, 2], corner_in.at[0, 0], gx + 1, me + 1, has_right & has_far, has_left & has_near),
        (edge_out.at[1, 2], corner_in.at[0, 1], gx - 1, me + 1, has_left & has_far, has_right & has_near),
        (edge_out.at[0, 0], corner_in.at[1, 0], gx + 1, me - 1, has_right & has_near, has_left & has_far),
        (edge_out.at[1, 0], corner_in.at[1, 1], gx - 1, me - 1, has_left & has_near, has_right & has_far),
        (edge_out.at[0], edge_in.at[0], gx + 1, me, has_right, has_left),
        (edge_out.at[1], edge_in.at[1], gx - 1, me, has_left, has_right),
    ]
    half = height // 2
    for h in range(2):
        rows = pl.ds(h * half, half)
        for fields, count, target in ((pl.ds(0, 2), 3, z01_in), (pl.ds(2, 2), 2, z23_in)):
            last = pl.ds(layers + 4 - count, count)
            table.append(
                (part.at[fields, last, rows], target.at[0, h], gx, me + 1, has_far, has_near)
            )
            table.append(
                (part.at[fields, pl.ds(0, count), rows], target.at[1, h], gx, me - 1, has_near, has_far)
            )

    def copy(number):
        source, target, gx_to, depth_to = table[number][:4]
        return pltpu.make_async_remote_copy(
            src_ref=source,
            dst_ref=target,
            send_sem=send_sem.at[number],
            recv_sem=recv_sem.at[number],
            device_id=(gx_to, depth_to),
            device_id_type=MESH,
        )

    for number in range(len(table)):
        @pl.when(table[number][4])
        def _():
            copy(number).start()

    for _, target, _, _, _, comes in table:
        @pl.when(jnp.logical_not(comes))
        def _():
            target[...] = jnp.zeros(target.shape, F32)

    for load in loads[4:]:
        load.wait()

    step_len = 0.25 / cells_z
    colours = pal.shape[1]
    spread = jnp.concatenate([pal[...], jnp.zeros((3, 128 - colours), F32)], axis=1)
    chosen = jnp.broadcast_to(pidx[...], (8, 128))
    entries = [ext[...] * step_len] + [
        jnp.take_along_axis(
            jnp.broadcast_to(spread[c : c + 1], (8, 128)), chosen, axis=1, mode="promise_in_bounds"
        )[0:1]
        for c in range(3)
    ]
    entries = jnp.concatenate(entries, axis=0)
    tab[0:4] = entries
    tab[4:8] = jnp.concatenate([entries[:, 1:], entries[:, :1]], axis=1) - entries

    zeros8 = jnp.zeros((layers + 4, 8, width), F32)
    for f in range(2):
        smooth[f, :, 0:8] = zeros8
        smooth[f, :, height + 8 : height + 16] = zeros8

    while 2 * reach < n_depth // 2:
        pl.semaphore_wait(known_sem.at[reach.bit_length() - 3], 2)
        reach *= 2
        know()

    def arrived(*numbers):
        for number in numbers:
            @pl.when(table[number][5])
            def _():
                copy(number).wait_recv()

    keep_near = jnp.where(has_near, 1.0, 0.0).astype(F32)
    keep_far = jnp.where(has_far, 1.0, 0.0).astype(F32)

    def turn_edges(k):
        for pair in range(2):
            edge = jnp.concatenate([edge_in[0, k, pair], edge_in[1, k, pair]], axis=0)
            if k != 1:
                edge += jnp.concatenate(
                    [corner_in[k // 2, 0, pair], corner_in[k // 2, 1, pair]], axis=0
                )
            edge = jnp.transpose(jnp.concatenate([edge, jnp.zeros((112, 128), F32)], axis=0))
            beside[k, pair, 0], beside[k, pair, 1] = halves(edge)

    def filter_width(k, pair, start, size):
        ys = slice(start, start + size)
        edges = [
            jnp.concatenate(
                [beside[k, pair, i, 32 * j + start : 32 * j + start + size] for j in range(4)], axis=0
            )
            for i in range(2)
        ]
        for f in range(2):
            field = 2 * pair + f
            body = [part[field, 4 * k + j, ys] for j in range(4)]
            came, count = (z01_in, 3) if pair == 0 else (z23_in, 2)
            if k == 0:
                for j in range(count):
                    body[4 - count + j] += came[0, start // half, f, j]
            if k == 2:
                for j in range(count):
                    body[j] += came[1, start // half, f, j]
            own = halves(jnp.concatenate(body, axis=0))
            high, low = [jnp.concatenate([own[i], edges[i]], axis=1) for i in range(2)]
            weights = xw[f] if pair == 0 else xw[f, :, :width]
            found = dot(high, weights) + dot(low, weights)
            here = found[:, :width].reshape(4, size, width)
            for j in range(4):
                layer = here[j]
                if pair == 0 and 4 * k + j == 1:
                    layer = layer * keep_near
                if pair == 0 and 4 * k + j == layers + 2:
                    layer = layer * keep_far
                smooth[field, 4 * k + j, 8 + start : 8 + start + size] = layer
            if pair == 0:
                slope[f, 4 * k : 4 * k + 4, ys] = found[:, width:].reshape(4, size, width)

    arrived(4, 5)
    turn_edges(1)
    filter_width(1, 0, 0, height)
    filter_width(1, 1, 0, height)
    arrived(0, 1, 2, 3)
    turn_edges(0)
    turn_edges(2)

    top = ext.shape[1] - 1

    def look(row, at, fraction):
        def pick(r):
            entry = jnp.broadcast_to(tab[r : r + 1], (layers * 8, 128))
            return jnp.take_along_axis(entry, at, axis=1, mode="promise_in_bounds")

        return (pick(row) + fraction * pick(row + 4)).reshape(layers, 8, width)

    def piece(to):
        return pltpu.make_async_remote_copy(
            src_ref=piece_out.at[to],
            dst_ref=piece_in.at[me],
            send_sem=piece_send,
            recv_sem=piece_recv,
            device_id=(gx, to),
            device_id_type=MESH,
        )

    for t in range(height // 8):
        if t < 2:
            arrived(6 + 4 * t, 7 + 4 * t)
            filter_width(0, 0, half * t, half)
            filter_width(2, 0, half * t, half)
            arrived(8 + 4 * t, 9 + 4 * t)
            filter_width(0, 1, half * t, half)
            filter_width(2, 1, half * t, half)
        here = pl.ds(8 * t + 8, 8)
        grads = []
        for f in range(2):
            grads.append(
                (
                    0.5 * (smooth[f, 3 : layers + 3, here] - smooth[f, 1 : layers + 1, here]),
                    0.5
                    * (
                        smooth[f, 2 : layers + 2, 8 * t + 9 : 8 * t + 17]
                        - smooth[f, 2 : layers + 2, 8 * t + 7 : 8 * t + 15]
                    ),
                    slope[f, 2 : layers + 2, pl.ds(8 * t, 8)],
                )
            )
        z0, y0, x0 = grads[0]
        z1, y1, x1 = grads[1]
        facing = LIGHT[0] * z0 + LIGHT[1] * y0 + LIGHT[2] * x0
        steep = z0 * z0 + y0 * y0 + x0 * x0
        shading = 0.35 + 0.65 * facing * facing / (steep + 0.05)
        warm = z1 * z1 + y1 * y1 + x1 * x1
        gain = 0.25 + 1.5 * warm / (warm + 0.1)
        place = (0.5 * top) * (1.0 + jnp.tanh(smooth[0, 2 : layers + 2, here]))
        at = jnp.clip(place.astype(jnp.int32), 0, top - 1)
        fraction = (place - at.astype(F32)).reshape(layers * 8, width)
        at = at.reshape(layers * 8, width)
        tau = look(0, at, fraction) * gain
        bright = (
            (1.0 + 0.5 * jnp.tanh(smooth[2, 2 : layers + 2, here]))
            * jnp.exp(0.5 * jnp.tanh(smooth[3, 2 : layers + 2, here]))
            * shading
        )
        absorbed = tau * (
            1.0
            - tau * (1 / 2)
            * (1.0 - tau * (1 / 3) * (1.0 - tau * (1 / 4) * (1.0 - tau * (1 / 5) * (1.0 - tau * (1 / 6)))))
        )
        opaque = jnp.zeros((8, width), F32)
        weights = []
        for z in range(layers):
            weight = absorbed[z] - absorbed[z] * opaque
            weights.append(weight[None])
            opaque = opaque + weight
        weight = jnp.concatenate(weights, axis=0) * bright
        for c in range(3):
            piece_out[pl.ds(8 * t, 8), c] = jnp.sum(weight * look(1 + c, at, fraction), axis=0)
        piece_out[pl.ds(8 * t, 8), 3] = opaque
        if t == 1:
            pl.semaphore_wait(known_sem.at[reach.bit_length() - 3], 2)

        @pl.loop(8 * t, 8 * t + 8)
        def _(to):
            @pl.when(to != me)
            def _():
                piece(to).start()

    own = pltpu.make_async_copy(piece_out.at[me], piece_in.at[me], piece_recv)
    own.start()
    for number in range(len(table)):
        @pl.when(table[number][4])
        def _():
            copy(number).wait_send()
    pltpu.make_async_copy(piece_in, piece_in, piece_recv).wait()
    others = piece_out.at[pl.ds(0, n_depth - 1)]
    pltpu.make_async_copy(others, others, piece_send).wait()

    group = n_depth // 8

    def over(nearer, farther):
        through = 1.0 - nearer[3]
        return [nearer[c] + through * farther[c] for c in range(4)]

    pieces = [
        [jnp.concatenate([piece_in[s * group + j, c : c + 1] for s in range(8)], axis=0) for c in range(4)]
        for j in range(group)
    ]
    total = pieces[0]
    for j in range(1, group):
        total = over(total, pieces[j])
    size = 8
    while size > 1:
        size //= 2
        nearer = [jnp.concatenate([v[2 * i : 2 * i + 1] for i in range(size)], axis=0) for v in total]
        farther = [jnp.concatenate([v[2 * i + 1 : 2 * i + 2] for i in range(size)], axis=0) for v in total]
        total = over(nearer, farther)
    out_ref[...] = jnp.concatenate(total, axis=0)


def solution(mesh):
    n_gx, n_depth = mesh.shape["gx"], mesh.shape["depth"]

    def per_device(volume, extinction, palette, palette_index):
        fields, layers, height, width = volume.shape
        entries = extinction.shape[0]
        colours = palette.shape[0]
        zy = depth_height_weights(layers, height)
        xw = width_weights(width)
        sel = edge_selector(width)
        anywhere = pl.BlockSpec(memory_space=pl.ANY)
        image = pl.pallas_call(
            functools.partial(kernel, n_gx, n_depth, layers * n_depth),
            out_shape=pltpu.VMEM((4, width), F32),
            in_specs=[anywhere] * 7,
            out_specs=pl.BlockSpec(memory_space=pltpu.VMEM),
            scratch_shapes=[
                pltpu.VMEM(volume.shape, F32),
                pltpu.VMEM((1, entries), F32),
                pltpu.VMEM((3, colours), F32),
                pltpu.VMEM((1, entries), jnp.int32),
                pltpu.VMEM(zy.shape, BF16),
                pltpu.VMEM(xw.shape[1:], BF16),
                pltpu.VMEM(sel.shape, BF16),
                pltpu.VMEM((8, entries), F32),
                pltpu.VMEM((fields, layers + 4, height, width), F32),
                pltpu.VMEM((2, 3, 2, 8, 128), F32),
                pltpu.VMEM((2, 3, 2, 8, 128), F32),
                pltpu.VMEM((2, 2, 2, 8, 128), F32),
                pltpu.VMEM((2, 2, 2, 3, height // 2, width), F32),
                pltpu.VMEM((2, 2, 2, 2, height // 2, width), F32),
                pltpu.VMEM((3, 2, 2, 128, 128), BF16),
                pltpu.VMEM((fields, layers + 4, height + 16, width), F32),
                pltpu.VMEM((2, layers + 4, height, width), F32),
                pltpu.VMEM((n_depth, 4, width), F32),
                pltpu.VMEM((n_depth, 4, width), F32),
                pltpu.SemaphoreType.DMA((8,)),
                pltpu.SemaphoreType.DMA((14,)),
                pltpu.SemaphoreType.DMA((14,)),
                pltpu.SemaphoreType.DMA,
                pltpu.SemaphoreType.DMA,
                pltpu.SemaphoreType.REGULAR((2,)),
            ],
            compiler_params=pltpu.CompilerParams(
                collective_id=0, has_side_effects=True, vmem_limit_bytes=VMEM_BYTES
            ),
        )(
            volume,
            extinction.reshape(1, entries),
            palette.T,
            palette_index.reshape(1, entries),
            jnp.asarray(zy),
            jnp.asarray(xw),
            jnp.asarray(sel),
        )
        return image.reshape(4, 1, width)

    placed = (P(None, "depth", None, "gx"), P(), P(), P())
    return jax.shard_map(
        per_device, mesh=mesh, in_specs=placed, out_specs=P(None, "gx", "depth"), check_vma=False
    )
```

```python
import functools

import jax
import jax.numpy as jnp
import ml_dtypes
import numpy as np
from jax import lax
from jax.experimental import pallas as pl
from jax.experimental.pallas import tpu as pltpu
from jax.sharding import PartitionSpec as P

TAPS = (0.0625, 0.25, 0.375, 0.25, 0.0625)
LIGHT = (0.64, 0.6, 0.48)
MESH = pl.DeviceIdType.MESH
FIRST = 8
VMEM_BYTES = 63 * 1024 * 1024
F32 = jnp.float32
BF16 = jnp.bfloat16


def tap(distance):
    return TAPS[distance + 2] if -2 <= distance <= 2 else 0.0


def depth_height_weights(layers, height):
    along_z = np.array([[tap(z - (i - 2)) for z in range(layers)] for i in range(layers + 4)])
    along_y = np.array([[tap(yy - y) for yy in range(height)] for y in range(height)])
    return np.kron(along_z, along_y).astype(ml_dtypes.bfloat16)


def width_weights(width):
    result = np.zeros((3, 2, 2 * width, 2 * width))
    for kind in range(3):
        cells = np.arange(-3, width + 3)
        full = np.array([[tap(c - x) for x in range(-1, width + 1)] for c in cells])
        if kind == 0:
            full[:3] = 0.0
            full[:, 0] = 0.0
        if kind == 2:
            full[-3:] = 0.0
            full[:, -1] = 0.0
        both = np.concatenate([full[:, 1:-1], 0.5 * (full[:, 2:] - full[:, :-2])], axis=1)
        for slot in range(2):
            result[kind, slot, :width] = both[3:-3]
            result[kind, slot, width + 4 * slot : width + 4 * slot + 3] = both[:3]
            result[kind, slot, width + 8 + 4 * slot : width + 8 + 4 * slot + 3] = both[-3:]
    return result.astype(ml_dtypes.bfloat16)


def edge_selector(width):
    result = np.zeros((16, 2 * width))
    for slot in range(2):
        for c in range(3):
            result[4 * slot + c, slot * width + width - 3 + c] = 1.0
            result[8 + 4 * slot + c, slot * width + c] = 1.0
    return result.astype(ml_dtypes.bfloat16)


def halves(values):
    high = values.astype(BF16)
    return high, (values - high.astype(F32)).astype(BF16)


def dot(a, b, dims=((1,), (0,))):
    return lax.dot_general(a, b, (dims, ((), ())), preferred_element_type=F32)


def kernel(
    n_gx, n_depth, cells_z,
    vol_hbm, ext_hbm, pal_hbm, pidx_hbm, zy_hbm, xw_hbm, sel_hbm,
    out_ref,
    vol, ext, pal, pidx, zy, xw, sel, tab,
    part, edge_out, edge_in, corner_in, z01_in, z23_in,
    beside, smooth, slope, piece_out, piece_in,
    load_sem, send_sem, recv_sem, piece_send, piece_recv, known_sem,
):
    gx = lax.axis_index("gx")
    me = lax.axis_index("depth")
    layers, height, width = vol.shape[1], vol.shape[2], vol.shape[3]
    has_left, has_right = gx > 0, gx < n_gx - 1
    has_near, has_far = me > 0, me < n_depth - 1

    kind = jnp.where(has_left, jnp.where(has_right, 1, 2), 0)
    loads = [
        pltpu.make_async_copy(vol_hbm.at[pl.ds(0, 2)], vol.at[pl.ds(0, 2)], load_sem.at[0]),
        pltpu.make_async_copy(zy_hbm, zy, load_sem.at[1]),
        pltpu.make_async_copy(vol_hbm.at[pl.ds(2, 2)], vol.at[pl.ds(2, 2)], load_sem.at[2]),
        pltpu.make_async_copy(sel_hbm, sel, load_sem.at[3]),
        pltpu.make_async_copy(xw_hbm.at[kind], xw, load_sem.at[4]),
        pltpu.make_async_copy(ext_hbm, ext, load_sem.at[5]),
        pltpu.make_async_copy(pal_hbm, pal, load_sem.at[6]),
        pltpu.make_async_copy(pidx_hbm, pidx, load_sem.at[7]),
    ]
    for load in loads[:2]:
        load.start()

    barrier = pltpu.get_barrier_semaphore()

    def around(distance):
        return lax.rem(me + n_depth + distance, n_depth)

    def greet(gx_to, depth_to, there):
        @pl.when(there)
        def _():
            pl.semaphore_signal(barrier, inc=1, device_id=(gx_to, depth_to), device_id_type=MESH)

    for step, there in ((1, has_far), (0, True)):
        greet(gx - 1, me + step, has_left & there)
        greet(gx + 1, me + step, has_right & there)
    reach = 4
    for distance in range(reach, 0, -1):
        for depth_to in (around(distance), around(-distance)):
            pl.semaphore_signal(barrier, inc=1, device_id=(gx, depth_to), device_id_type=MESH)
    for load in loads[2:]:
        load.start()

    @pl.when(me < FIRST)
    def _():
        @pl.loop(reach + 1, n_depth - reach)
        def _(distance):
            pl.semaphore_signal(
                barrier, inc=1, device_id=(gx, around(distance)), device_id_type=MESH
            )

    n_first = 0
    for device in range(FIRST):
        apart = lax.rem(me + n_depth - device, n_depth)
        n_first += ((apart > reach) & (apart < n_depth - reach)).astype(jnp.int32)

    def know():
        for depth_to in (around(reach), around(-reach)):
            pl.semaphore_signal(
                known_sem.at[reach.bit_length() - 3], inc=1, device_id=(gx, depth_to), device_id_type=MESH
            )

    def filter_own(pair):
        raw = jnp.concatenate(
            [vol[2 * pair + f].reshape(layers * height, width) for f in range(2)], axis=1
        )
        high, low = halves(raw)
        spread = dot(zy[...], high) + dot(zy[...], low)
        for f in range(2):
            part[2 * pair + f] = spread[:, f * width : (f + 1) * width].reshape(
                layers + 4, height, width
            )
        high, low = halves(spread)
        edges = dot(sel[...], high, ((1,), (1,))) + dot(sel[...], low, ((1,), (1,)))
        for side in range(2):
            for k in range(3):
                edge_out[side, k, pair] = edges[
                    8 * side : 8 * side + 8, 128 * k : 128 * k + 128
                ]

    for load in (loads[0], loads[1], loads[3]):
        load.wait()
    filter_own(0)
    loads[2].wait()
    filter_own(1)
    n_sides = has_left.astype(jnp.int32) + has_right.astype(jnp.int32)
    n_rows = 1 + has_near.astype(jnp.int32)
    pl.semaphore_wait(barrier, 2 * reach + n_sides * n_rows + n_first)
    know()

    table = [
        (edge_out.at[0, pl.ds(0, 2)], corner_in.at[0], gx + 1, me - 1, has_right & has_near, has_left & has_far),
        (edge_out.at[1, pl.ds(0, 2)], corner_in.at[1], gx - 1, me - 1, has_left & has_near, has_right & has_far),
        (edge_out.at[0], edge_in.at[0], gx + 1, me, has_right, has_left),
        (edge_out.at[1], edge_in.at[1], gx - 1, me, has_left, has_right),
    ]
    half = height // 2
    for h in range(2):
        rows = pl.ds(h * half, half)
        for fields, count, target in ((pl.ds(0, 2), 6, z01_in), (pl.ds(2, 2), 5, z23_in)):
            table.append(
                (part.at[fields, pl.ds(0, count), rows], target.at[h], gx, me - 1, has_near, has_far)
            )

    def copy(number):
        source, target, gx_to, depth_to = table[number][:4]
        return pltpu.make_async_remote_copy(
            src_ref=source,
            dst_ref=target,
            send_sem=send_sem.at[number],
            recv_sem=recv_sem.at[number],
            device_id=(gx_to, depth_to),
            device_id_type=MESH,
        )

    for number in range(len(table)):
        @pl.when(table[number][4])
        def _():
            copy(number).start()

    for _, target, _, _, _, comes in table:
        @pl.when(jnp.logical_not(comes))
        def _():
            target[...] = jnp.zeros(target.shape, F32)

    for load in loads[4:]:
        load.wait()

    step_len = 0.25 / cells_z
    colours = pal.shape[1]
    spread = jnp.concatenate([pal[...], jnp.zeros((3, 128 - colours), F32)], axis=1)
    chosen = jnp.broadcast_to(pidx[...], (8, 128))
    entries = [ext[...] * step_len] + [
        jnp.take_along_axis(
            jnp.broadcast_to(spread[c : c + 1], (8, 128)), chosen, axis=1, mode="promise_in_bounds"
        )[0:1]
        for c in range(3)
    ]
    entries = jnp.concatenate(entries, axis=0)
    tab[0:4] = entries
    tab[4:8] = jnp.concatenate([entries[:, 1:], entries[:, :1]], axis=1) - entries

    zeros8 = jnp.zeros((layers + 8, 8, width), F32)
    for f in range(2):
        smooth[f, :, 0:8] = zeros8
        smooth[f, :, height + 8 : height + 16] = zeros8

    while 2 * reach < n_depth // 2:
        pl.semaphore_wait(known_sem.at[reach.bit_length() - 3], 2)
        reach *= 2
        know()

    def arrived(*numbers):
        for number in numbers:
            @pl.when(table[number][5])
            def _():
                copy(number).wait_recv()

    keep_near = jnp.where(has_near, 1.0, 0.0).astype(F32)
    keep_far = jnp.where(has_far, 1.0, 0.0).astype(F32)

    def turn_edges(k):
        for pair in range(2):
            edge = jnp.zeros((16, 128), F32)
            if k < 3:
                edge += jnp.concatenate([edge_in[0, k, pair], edge_in[1, k, pair]], axis=0)
            if k >= 2:
                edge += jnp.concatenate(
                    [corner_in[0, k - 2, pair], corner_in[1, k - 2, pair]], axis=0
                )
            edge = jnp.transpose(jnp.concatenate([edge, jnp.zeros((112, 128), F32)], axis=0))
            beside[k, pair, 0], beside[k, pair, 1] = halves(edge)

    def filter_width(ks, start, size):
        ys = slice(start, start + size)
        blocks = [(k, pair) for k in ks for pair in range(2)]
        edges = [
            jnp.concatenate(
                [
                    beside[k, pair, i, 32 * j + start : 32 * j + start + size]
                    for k, pair in blocks
                    for j in range(4)
                ],
                axis=0,
            )
            for i in range(2)
        ]
        for f in range(2):
            body = []
            for k, pair in blocks:
                came, count = (z01_in, 6) if pair == 0 else (z23_in, 5)
                layer = []
                for j in range(4):
                    terms = []
                    if 4 * k + j < layers + 4:
                        terms.append(part[2 * pair + f, 4 * k + j, ys])
                    if 0 <= 4 * k + j - layers < count:
                        terms.append(came[start // half, f, 4 * k + j - layers])
                    layer.append(sum(terms) if terms else jnp.zeros((size, width), F32))
                body += layer
            own = halves(jnp.concatenate(body, axis=0))
            both = jnp.concatenate(
                [jnp.concatenate([own[i], edges[i]], axis=1) for i in range(2)], axis=0
            )
            found = dot(both, xw[f])
            found = found[: found.shape[0] // 2] + found[found.shape[0] // 2 :]
            for at, (k, pair) in enumerate(blocks):
                here = found[4 * size * at : 4 * size * (at + 1)]
                if pair == 0:
                    slope[f, 4 * k : 4 * k + 4, ys] = here[:, width:].reshape(4, size, width)
                here = here[:, :width].reshape(4, size, width)
                for j in range(4):
                    layer = here[j]
                    if pair == 0 and 4 * k + j == 1:
                        layer = layer * keep_near
                    if pair == 0 and 4 * k + j == layers + 2:
                        layer = layer * keep_far
                    smooth[2 * pair + f, 4 * k + j, 8 + start : 8 + start + size] = layer

    arrived(2, 3)
    turn_edges(0)
    turn_edges(1)
    filter_width((0, 1), 0, height)
    arrived(0, 1)
    turn_edges(2)
    turn_edges(3)

    count = layers + 3
    top = ext.shape[1] - 1

    def look(row, at, fraction):
        def pick(r):
            entry = jnp.broadcast_to(tab[r : r + 1], (count * 8, 128))
            return jnp.take_along_axis(entry, at, axis=1, mode="promise_in_bounds")

        return (pick(row) + fraction * pick(row + 4)).reshape(count, 8, width)

    def piece(to):
        return pltpu.make_async_remote_copy(
            src_ref=piece_out.at[to],
            dst_ref=piece_in.at[me],
            send_sem=piece_send,
            recv_sem=piece_recv,
            device_id=(gx, to),
            device_id_type=MESH,
        )

    for t in range(height // 8):
        if t < 2:
            arrived(4 + 2 * t, 5 + 2 * t)
            filter_width((2, 3), half * t, half)
        here = pl.ds(8 * t + 8, 8)
        grads = []
        for f in range(2):
            grads.append(
                (
                    0.5 * (smooth[f, 3 : count + 3, here] - smooth[f, 1 : count + 1, here]),
                    0.5
                    * (
                        smooth[f, 2 : count + 2, 8 * t + 9 : 8 * t + 17]
                        - smooth[f, 2 : count + 2, 8 * t + 7 : 8 * t + 15]
                    ),
                    slope[f, 2 : count + 2, pl.ds(8 * t, 8)],
                )
            )
        z0, y0, x0 = grads[0]
        z1, y1, x1 = grads[1]
        facing = LIGHT[0] * z0 + LIGHT[1] * y0 + LIGHT[2] * x0
        steep = z0 * z0 + y0 * y0 + x0 * x0
        shading = 0.35 + 0.65 * facing * facing / (steep + 0.05)
        warm = z1 * z1 + y1 * y1 + x1 * x1
        gain = 0.25 + 1.5 * warm / (warm + 0.1)
        place = (0.5 * top) * (1.0 + jnp.tanh(smooth[0, 2 : count + 2, here]))
        at = jnp.clip(place.astype(jnp.int32), 0, top - 1)
        fraction = (place - at.astype(F32)).reshape(count * 8, width)
        at = at.reshape(count * 8, width)
        tau = look(0, at, fraction) * gain
        bright = (
            (1.0 + 0.5 * jnp.tanh(smooth[2, 2 : count + 2, here]))
            * jnp.exp(0.5 * jnp.tanh(smooth[3, 2 : count + 2, here]))
            * shading
        )
        absorbed = tau * (
            1.0
            - tau * (1 / 2)
            * (1.0 - tau * (1 / 3) * (1.0 - tau * (1 / 4) * (1.0 - tau * (1 / 5) * (1.0 - tau * (1 / 6)))))
        )
        opaque = jnp.zeros((8, width), F32)
        weights = []
        for z in range(count):
            here = absorbed[z]
            if z < 3:
                here = here * (1.0 - keep_near)
            if z >= layers:
                here = here * keep_far
            weight = here - here * opaque
            weights.append(weight[None])
            opaque = opaque + weight
        weight = jnp.concatenate(weights, axis=0) * bright
        for c in range(3):
            piece_out[pl.ds(8 * t, 8), c] = jnp.sum(weight * look(1 + c, at, fraction), axis=0)
        piece_out[pl.ds(8 * t, 8), 3] = opaque
        if t == 1:
            pl.semaphore_wait(known_sem.at[reach.bit_length() - 3], 2)

        @pl.loop(8 * t, 8 * t + 8)
        def _(to):
            @pl.when(to != me)
            def _():
                piece(to).start()

    own = pltpu.make_async_copy(piece_out.at[me], piece_in.at[me], piece_recv)
    own.start()
    for number in range(len(table)):
        @pl.when(table[number][4])
        def _():
            copy(number).wait_send()
    pltpu.make_async_copy(piece_in, piece_in, piece_recv).wait()
    others = piece_out.at[pl.ds(0, n_depth - 1)]
    pltpu.make_async_copy(others, others, piece_send).wait()

    group = n_depth // 8

    def over(nearer, farther):
        through = 1.0 - nearer[3]
        return [nearer[c] + through * farther[c] for c in range(4)]

    pieces = [
        [jnp.concatenate([piece_in[s * group + j, c : c + 1] for s in range(8)], axis=0) for c in range(4)]
        for j in range(group)
    ]
    total = pieces[0]
    for j in range(1, group):
        total = over(total, pieces[j])
    size = 8
    while size > 1:
        size //= 2
        nearer = [jnp.concatenate([v[2 * i : 2 * i + 1] for i in range(size)], axis=0) for v in total]
        farther = [jnp.concatenate([v[2 * i + 1 : 2 * i + 2] for i in range(size)], axis=0) for v in total]
        total = over(nearer, farther)
    out_ref[...] = jnp.concatenate(total, axis=0)


def solution(mesh):
    n_gx, n_depth = mesh.shape["gx"], mesh.shape["depth"]

    def per_device(volume, extinction, palette, palette_index):
        fields, layers, height, width = volume.shape
        entries = extinction.shape[0]
        colours = palette.shape[0]
        zy = depth_height_weights(layers, height)
        xw = width_weights(width)
        sel = edge_selector(width)
        anywhere = pl.BlockSpec(memory_space=pl.ANY)
        image = pl.pallas_call(
            functools.partial(kernel, n_gx, n_depth, layers * n_depth),
            out_shape=pltpu.VMEM((4, width), F32),
            in_specs=[anywhere] * 7,
            out_specs=pl.BlockSpec(memory_space=pltpu.VMEM),
            scratch_shapes=[
                pltpu.VMEM(volume.shape, F32),
                pltpu.VMEM((1, entries), F32),
                pltpu.VMEM((3, colours), F32),
                pltpu.VMEM((1, entries), jnp.int32),
                pltpu.VMEM(zy.shape, BF16),
                pltpu.VMEM(xw.shape[1:], BF16),
                pltpu.VMEM(sel.shape, BF16),
                pltpu.VMEM((8, entries), F32),
                pltpu.VMEM((fields, layers + 4, height, width), F32),
                pltpu.VMEM((2, 3, 2, 8, 128), F32),
                pltpu.VMEM((2, 3, 2, 8, 128), F32),
                pltpu.VMEM((2, 2, 2, 8, 128), F32),
                pltpu.VMEM((2, 2, 6, height // 2, width), F32),
                pltpu.VMEM((2, 2, 5, height // 2, width), F32),
                pltpu.VMEM((4, 2, 2, 128, 128), BF16),
                pltpu.VMEM((fields, layers + 8, height + 16, width), F32),
                pltpu.VMEM((2, layers + 8, height, width), F32),
                pltpu.VMEM((n_depth, 4, width), F32),
                pltpu.VMEM((n_depth, 4, width), F32),
                pltpu.SemaphoreType.DMA((8,)),
                pltpu.SemaphoreType.DMA((8,)),
                pltpu.SemaphoreType.DMA((8,)),
                pltpu.SemaphoreType.DMA,
                pltpu.SemaphoreType.DMA,
                pltpu.SemaphoreType.REGULAR((2,)),
            ],
            compiler_params=pltpu.CompilerParams(
                collective_id=0, has_side_effects=True, vmem_limit_bytes=VMEM_BYTES
            ),
        )(
            volume,
            extinction.reshape(1, entries),
            palette.T,
            palette_index.reshape(1, entries),
            jnp.asarray(zy),
            jnp.asarray(xw),
            jnp.asarray(sel),
        )
        return image.reshape(4, 1, width)

    placed = (P(None, "depth", None, "gx"), P(), P(), P())
    return jax.shard_map(
        per_device, mesh=mesh, in_specs=placed, out_specs=P(None, "gx", "depth"), check_vma=False
    )
```

```python
import functools

import jax
import jax.numpy as jnp
import ml_dtypes
import numpy as np
from jax import lax
from jax.experimental import pallas as pl
from jax.experimental.pallas import tpu as pltpu
from jax.sharding import PartitionSpec as P

TAPS = (0.0625, 0.25, 0.375, 0.25, 0.0625)
LIGHT = (0.64, 0.6, 0.48)
MESH = pl.DeviceIdType.MESH
FIRST = 8
VMEM_BYTES = 63 * 1024 * 1024
F32 = jnp.float32
BF16 = jnp.bfloat16


def tap(distance):
    return TAPS[distance + 2] if -2 <= distance <= 2 else 0.0


def depth_height_weights(layers, height):
    along_z = np.array([[tap(z - (i - 2)) for z in range(layers)] for i in range(layers + 4)])
    along_y = np.array([[tap(yy - y) for yy in range(height)] for y in range(height)])
    return np.kron(along_z, along_y).astype(ml_dtypes.bfloat16)


def width_weights(width):
    result = np.zeros((3, 2, 2 * width, 2 * width))
    for kind in range(3):
        cells = np.arange(-3, width + 3)
        full = np.array([[tap(c - x) for x in range(-1, width + 1)] for c in cells])
        if kind == 0:
            full[:3] = 0.0
            full[:, 0] = 0.0
        if kind == 2:
            full[-3:] = 0.0
            full[:, -1] = 0.0
        both = np.concatenate([full[:, 1:-1], 0.5 * (full[:, 2:] - full[:, :-2])], axis=1)
        for slot in range(2):
            result[kind, slot, :width] = both[3:-3]
            result[kind, slot, width + 4 * slot : width + 4 * slot + 3] = both[:3]
            result[kind, slot, width + 8 + 4 * slot : width + 8 + 4 * slot + 3] = both[-3:]
    return result.astype(ml_dtypes.bfloat16)


def edge_selector(width):
    result = np.zeros((16, 2 * width))
    for slot in range(2):
        for c in range(3):
            result[4 * slot + c, slot * width + width - 3 + c] = 1.0
            result[8 + 4 * slot + c, slot * width + c] = 1.0
    return result.astype(ml_dtypes.bfloat16)


def halves(values):
    high = values.astype(BF16)
    return high, (values - high.astype(F32)).astype(BF16)


def dot(a, b, dims=((1,), (0,))):
    return lax.dot_general(a, b, (dims, ((), ())), preferred_element_type=F32)


def kernel(
    n_gx, n_depth, cells_z,
    vol_hbm, ext_hbm, pal_hbm, pidx_hbm, zy_hbm, xw_hbm, sel_hbm,
    out_ref,
    vol, ext, pal, pidx, zy, xw, sel, tab,
    part, edge_out, edge_in, corner_in, z01_in, z23_in,
    beside, smooth, slope, piece_out, piece_in,
    load_sem, send_sem, recv_sem, piece_send, piece_recv, known_sem,
):
    gx = lax.axis_index("gx")
    me = lax.axis_index("depth")
    layers, height, width = vol.shape[1], vol.shape[2], vol.shape[3]
    has_left, has_right = gx > 0, gx < n_gx - 1
    has_near, has_far = me > 0, me < n_depth - 1

    kind = jnp.where(has_left, jnp.where(has_right, 1, 2), 0)
    loads = [
        pltpu.make_async_copy(vol_hbm.at[pl.ds(0, 2)], vol.at[pl.ds(0, 2)], load_sem.at[0]),
        pltpu.make_async_copy(zy_hbm, zy, load_sem.at[1]),
        pltpu.make_async_copy(vol_hbm.at[pl.ds(2, 2)], vol.at[pl.ds(2, 2)], load_sem.at[2]),
        pltpu.make_async_copy(sel_hbm, sel, load_sem.at[3]),
        pltpu.make_async_copy(xw_hbm.at[kind], xw, load_sem.at[4]),
        pltpu.make_async_copy(ext_hbm, ext, load_sem.at[5]),
        pltpu.make_async_copy(pal_hbm, pal, load_sem.at[6]),
        pltpu.make_async_copy(pidx_hbm, pidx, load_sem.at[7]),
    ]
    for load in loads[:2]:
        load.start()

    barrier = pltpu.get_barrier_semaphore()

    def around(distance):
        return lax.rem(me + n_depth + distance, n_depth)

    def greet(gx_to, depth_to, there):
        @pl.when(there)
        def _():
            pl.semaphore_signal(barrier, inc=1, device_id=(gx_to, depth_to), device_id_type=MESH)

    for step, there in ((1, has_far), (0, True)):
        greet(gx - 1, me + step, has_left & there)
        greet(gx + 1, me + step, has_right & there)
    reach = 4
    for distance in range(reach, 0, -1):
        for depth_to in (around(distance), around(-distance)):
            pl.semaphore_signal(barrier, inc=1, device_id=(gx, depth_to), device_id_type=MESH)
    for load in loads[2:]:
        load.start()

    @pl.when(me < FIRST)
    def _():
        @pl.loop(reach + 1, n_depth - reach)
        def _(distance):
            pl.semaphore_signal(
                barrier, inc=1, device_id=(gx, around(distance)), device_id_type=MESH
            )

    n_first = 0
    for device in range(FIRST):
        apart = lax.rem(me + n_depth - device, n_depth)
        n_first += ((apart > reach) & (apart < n_depth - reach)).astype(jnp.int32)

    def know():
        for depth_to in (around(reach), around(-reach)):
            pl.semaphore_signal(
                known_sem.at[reach.bit_length() - 3], inc=1, device_id=(gx, depth_to), device_id_type=MESH
            )

    def filter_own(pair):
        raw = jnp.concatenate(
            [vol[2 * pair + f].reshape(layers * height, width) for f in range(2)], axis=1
        )
        high, low = halves(raw)
        spread = dot(zy[...], high) + dot(zy[...], low)
        for f in range(2):
            part[2 * pair + f] = spread[:, f * width : (f + 1) * width].reshape(
                layers + 4, height, width
            )
        high, low = halves(spread)
        edges = dot(sel[...], high, ((1,), (1,))) + dot(sel[...], low, ((1,), (1,)))
        for side in range(2):
            for k in range(3):
                edge_out[side, k, pair] = edges[
                    8 * side : 8 * side + 8, 128 * k : 128 * k + 128
                ]

    for load in (loads[0], loads[1], loads[3]):
        load.wait()
    filter_own(0)
    loads[2].wait()
    filter_own(1)
    n_sides = has_left.astype(jnp.int32) + has_right.astype(jnp.int32)
    n_rows = 1 + has_near.astype(jnp.int32)
    pl.semaphore_wait(barrier, 2 * reach + n_sides * n_rows + n_first)
    know()

    table = [
        (edge_out.at[0, pl.ds(0, 2)], corner_in.at[0], gx + 1, me - 1, has_right & has_near, has_left & has_far),
        (edge_out.at[1, pl.ds(0, 2)], corner_in.at[1], gx - 1, me - 1, has_left & has_near, has_right & has_far),
        (edge_out.at[0], edge_in.at[0], gx + 1, me, has_right, has_left),
        (edge_out.at[1], edge_in.at[1], gx - 1, me, has_left, has_right),
    ]
    half = height // 2
    for h in range(2):
        rows = pl.ds(h * half, half)
        for fields, count, target in ((pl.ds(0, 2), 6, z01_in), (pl.ds(2, 2), 5, z23_in)):
            table.append(
                (part.at[fields, pl.ds(0, count), rows], target.at[h], gx, me - 1, has_near, has_far)
            )

    def copy(number):
        source, target, gx_to, depth_to = table[number][:4]
        return pltpu.make_async_remote_copy(
            src_ref=source,
            dst_ref=target,
            send_sem=send_sem.at[number],
            recv_sem=recv_sem.at[number],
            device_id=(gx_to, depth_to),
            device_id_type=MESH,
        )

    for number in range(len(table)):
        @pl.when(table[number][4])
        def _():
            copy(number).start()

    for _, target, _, _, _, comes in table:
        @pl.when(jnp.logical_not(comes))
        def _():
            target[...] = jnp.zeros(target.shape, F32)

    for load in loads[4:]:
        load.wait()

    step_len = 0.25 / cells_z
    colours = pal.shape[1]
    spread = jnp.concatenate([pal[...], jnp.zeros((3, 128 - colours), F32)], axis=1)
    chosen = jnp.broadcast_to(pidx[...], (8, 128))
    entries = [ext[...] * step_len] + [
        jnp.take_along_axis(
            jnp.broadcast_to(spread[c : c + 1], (8, 128)), chosen, axis=1, mode="promise_in_bounds"
        )[0:1]
        for c in range(3)
    ]
    entries = jnp.concatenate(entries, axis=0)
    tab[0:4] = entries
    tab[4:8] = jnp.concatenate([entries[:, 1:], entries[:, :1]], axis=1) - entries

    zeros8 = jnp.zeros((layers + 8, 8, width), F32)
    for f in range(2):
        smooth[f, :, 0:8] = zeros8
        smooth[f, :, height + 8 : height + 16] = zeros8

    while 2 * reach < n_depth // 2:
        pl.semaphore_wait(known_sem.at[reach.bit_length() - 3], 2)
        reach *= 2
        know()

    def arrived(*numbers):
        for number in numbers:
            @pl.when(table[number][5])
            def _():
                copy(number).wait_recv()

    keep_near = jnp.where(has_near, 1.0, 0.0).astype(F32)
    keep_far = jnp.where(has_far, 1.0, 0.0).astype(F32)

    def turn_edges(k):
        for pair in range(2):
            edge = jnp.zeros((16, 128), F32)
            if k < 3:
                edge += jnp.concatenate([edge_in[0, k, pair], edge_in[1, k, pair]], axis=0)
            if k >= 2:
                edge += jnp.concatenate(
                    [corner_in[0, k - 2, pair], corner_in[1, k - 2, pair]], axis=0
                )
            edge = jnp.transpose(jnp.concatenate([edge, jnp.zeros((112, 128), F32)], axis=0))
            beside[k, pair, 0], beside[k, pair, 1] = halves(edge)

    def filter_width(ks, start, size):
        ys = slice(start, start + size)
        blocks = [(k, pair) for k in ks for pair in range(2)]
        edges = [
            jnp.concatenate(
                [
                    beside[k, pair, i, 32 * j + start : 32 * j + start + size]
                    for k, pair in blocks
                    for j in range(4)
                ],
                axis=0,
            )
            for i in range(2)
        ]
        for f in range(2):
            body = []
            for k, pair in blocks:
                came, count = (z01_in, 6) if pair == 0 else (z23_in, 5)
                layer = []
                for j in range(4):
                    terms = []
                    if 4 * k + j < layers + 4:
                        terms.append(part[2 * pair + f, 4 * k + j, ys])
                    if 0 <= 4 * k + j - layers < count:
                        terms.append(came[start // half, f, 4 * k + j - layers])
                    layer.append(sum(terms) if terms else jnp.zeros((size, width), F32))
                body += layer
            own = halves(jnp.concatenate(body, axis=0))
            both = jnp.concatenate(
                [jnp.concatenate([own[i], edges[i]], axis=1) for i in range(2)], axis=0
            )
            found = dot(both, xw[f])
            found = found[: found.shape[0] // 2] + found[found.shape[0] // 2 :]
            for at, (k, pair) in enumerate(blocks):
                here = found[4 * size * at : 4 * size * (at + 1)]
                if pair == 0:
                    slope[f, 4 * k : 4 * k + 4, ys] = here[:, width:].reshape(4, size, width)
                here = here[:, :width].reshape(4, size, width)
                for j in range(4):
                    layer = here[j]
                    if pair == 0 and 4 * k + j == 1:
                        layer = layer * keep_near
                    if pair == 0 and 4 * k + j == layers + 2:
                        layer = layer * keep_far
                    smooth[2 * pair + f, 4 * k + j, 8 + start : 8 + start + size] = layer

    arrived(2, 3)
    turn_edges(0)
    turn_edges(1)
    filter_width((0, 1), 0, half)
    arrived(0, 1)
    turn_edges(2)
    turn_edges(3)

    count = layers + 3
    top = ext.shape[1] - 1

    def look(row, at, fraction):
        def pick(r):
            entry = jnp.broadcast_to(tab[r : r + 1], (count * 8, 128))
            return jnp.take_along_axis(entry, at, axis=1, mode="promise_in_bounds")

        return (pick(row) + fraction * pick(row + 4)).reshape(count, 8, width)

    def piece(to):
        return pltpu.make_async_remote_copy(
            src_ref=piece_out.at[to],
            dst_ref=piece_in.at[me],
            send_sem=piece_send,
            recv_sem=piece_recv,
            device_id=(gx, to),
            device_id_type=MESH,
        )

    for t in range(height // 8):
        if t < 2:
            arrived(4 + 2 * t, 5 + 2 * t)
            filter_width((2, 3) if t == 0 else (0, 1, 2, 3), half * t, half)
        here = pl.ds(8 * t + 8, 8)
        grads = []
        for f in range(2):
            grads.append(
                (
                    0.5 * (smooth[f, 3 : count + 3, here] - smooth[f, 1 : count + 1, here]),
                    0.5
                    * (
                        smooth[f, 2 : count + 2, 8 * t + 9 : 8 * t + 17]
                        - smooth[f, 2 : count + 2, 8 * t + 7 : 8 * t + 15]
                    ),
                    slope[f, 2 : count + 2, pl.ds(8 * t, 8)],
                )
            )
        z0, y0, x0 = grads[0]
        z1, y1, x1 = grads[1]
        facing = LIGHT[0] * z0 + LIGHT[1] * y0 + LIGHT[2] * x0
        steep = z0 * z0 + y0 * y0 + x0 * x0
        shading = 0.35 + 0.65 * facing * facing / (steep + 0.05)
        warm = z1 * z1 + y1 * y1 + x1 * x1
        gain = 0.25 + 1.5 * warm / (warm + 0.1)
        place = (0.5 * top) * (1.0 + jnp.tanh(smooth[0, 2 : count + 2, here]))
        at = jnp.clip(place.astype(jnp.int32), 0, top - 1)
        fraction = (place - at.astype(F32)).reshape(count * 8, width)
        at = at.reshape(count * 8, width)
        tau = look(0, at, fraction) * gain
        bright = (
            (1.0 + 0.5 * jnp.tanh(smooth[2, 2 : count + 2, here]))
            * jnp.exp(0.5 * jnp.tanh(smooth[3, 2 : count + 2, here]))
            * shading
        )
        absorbed = tau * (
            1.0
            - tau * (1 / 2)
            * (1.0 - tau * (1 / 3) * (1.0 - tau * (1 / 4) * (1.0 - tau * (1 / 5) * (1.0 - tau * (1 / 6)))))
        )
        opaque = jnp.zeros((8, width), F32)
        weights = []
        for z in range(count):
            here = absorbed[z]
            if z < 3:
                here = here * (1.0 - keep_near)
            if z >= layers:
                here = here * keep_far
            weight = here - here * opaque
            weights.append(weight[None])
            opaque = opaque + weight
        weight = jnp.concatenate(weights, axis=0) * bright
        for c in range(3):
            piece_out[pl.ds(8 * t, 8), c] = jnp.sum(weight * look(1 + c, at, fraction), axis=0)
        piece_out[pl.ds(8 * t, 8), 3] = opaque
        if t == 1:
            pl.semaphore_wait(known_sem.at[reach.bit_length() - 3], 2)

        @pl.loop(8 * t, 8 * t + 8)
        def _(to):
            @pl.when(to != me)
            def _():
                piece(to).start()

    own = pltpu.make_async_copy(piece_out.at[me], piece_in.at[me], piece_recv)
    own.start()
    for number in range(len(table)):
        @pl.when(table[number][4])
        def _():
            copy(number).wait_send()
    pltpu.make_async_copy(piece_in, piece_in, piece_recv).wait()
    others = piece_out.at[pl.ds(0, n_depth - 1)]
    pltpu.make_async_copy(others, others, piece_send).wait()

    group = n_depth // 8

    def over(nearer, farther):
        through = 1.0 - nearer[3]
        return [nearer[c] + through * farther[c] for c in range(4)]

    pieces = [
        [jnp.concatenate([piece_in[s * group + j, c : c + 1] for s in range(8)], axis=0) for c in range(4)]
        for j in range(group)
    ]
    total = pieces[0]
    for j in range(1, group):
        total = over(total, pieces[j])
    size = 8
    while size > 1:
        size //= 2
        nearer = [jnp.concatenate([v[2 * i : 2 * i + 1] for i in range(size)], axis=0) for v in total]
        farther = [jnp.concatenate([v[2 * i + 1 : 2 * i + 2] for i in range(size)], axis=0) for v in total]
        total = over(nearer, farther)
    out_ref[...] = jnp.concatenate(total, axis=0)


def solution(mesh):
    n_gx, n_depth = mesh.shape["gx"], mesh.shape["depth"]

    def per_device(volume, extinction, palette, palette_index):
        fields, layers, height, width = volume.shape
        entries = extinction.shape[0]
        colours = palette.shape[0]
        zy = depth_height_weights(layers, height)
        xw = width_weights(width)
        sel = edge_selector(width)
        anywhere = pl.BlockSpec(memory_space=pl.ANY)
        image = pl.pallas_call(
            functools.partial(kernel, n_gx, n_depth, layers * n_depth),
            out_shape=pltpu.VMEM((4, width), F32),
            in_specs=[anywhere] * 7,
            out_specs=pl.BlockSpec(memory_space=pltpu.VMEM),
            scratch_shapes=[
                pltpu.VMEM(volume.shape, F32),
                pltpu.VMEM((1, entries), F32),
                pltpu.VMEM((3, colours), F32),
                pltpu.VMEM((1, entries), jnp.int32),
                pltpu.VMEM(zy.shape, BF16),
                pltpu.VMEM(xw.shape[1:], BF16),
                pltpu.VMEM(sel.shape, BF16),
                pltpu.VMEM((8, entries), F32),
                pltpu.VMEM((fields, layers + 4, height, width), F32),
                pltpu.VMEM((2, 3, 2, 8, 128), F32),
                pltpu.VMEM((2, 3, 2, 8, 128), F32),
                pltpu.VMEM((2, 2, 2, 8, 128), F32),
                pltpu.VMEM((2, 2, 6, height // 2, width), F32),
                pltpu.VMEM((2, 2, 5, height // 2, width), F32),
                pltpu.VMEM((4, 2, 2, 128, 128), BF16),
                pltpu.VMEM((fields, layers + 8, height + 16, width), F32),
                pltpu.VMEM((2, layers + 8, height, width), F32),
                pltpu.VMEM((n_depth, 4, width), F32),
                pltpu.VMEM((n_depth, 4, width), F32),
                pltpu.SemaphoreType.DMA((8,)),
                pltpu.SemaphoreType.DMA((8,)),
                pltpu.SemaphoreType.DMA((8,)),
                pltpu.SemaphoreType.DMA,
                pltpu.SemaphoreType.DMA,
                pltpu.SemaphoreType.REGULAR((2,)),
            ],
            compiler_params=pltpu.CompilerParams(
                collective_id=0, has_side_effects=True, vmem_limit_bytes=VMEM_BYTES
            ),
        )(
            volume,
            extinction.reshape(1, entries),
            palette.T,
            palette_index.reshape(1, entries),
            jnp.asarray(zy),
            jnp.asarray(xw),
            jnp.asarray(sel),
        )
        return image.reshape(4, 1, width)

    placed = (P(None, "depth", None, "gx"), P(), P(), P())
    return jax.shard_map(
        per_device, mesh=mesh, in_specs=placed, out_specs=P(None, "gx", "depth"), check_vma=False
    )
```

```python
import functools

import jax
import jax.numpy as jnp
import ml_dtypes
import numpy as np
from jax import lax
from jax.experimental import pallas as pl
from jax.experimental.pallas import tpu as pltpu
from jax.sharding import PartitionSpec as P

TAPS = (0.0625, 0.25, 0.375, 0.25, 0.0625)
LIGHT = (0.64, 0.6, 0.48)
MESH = pl.DeviceIdType.MESH
FIRST = 8
VMEM_BYTES = 63 * 1024 * 1024
F32 = jnp.float32
BF16 = jnp.bfloat16


def tap(distance):
    return TAPS[distance + 2] if -2 <= distance <= 2 else 0.0


def depth_height_weights(layers, height):
    along_z = np.array([[tap(z - (i - 2)) for z in range(layers)] for i in range(layers + 4)])
    along_y = np.array([[tap(yy - y) for yy in range(height)] for y in range(height)])
    return np.kron(along_z, along_y).astype(ml_dtypes.bfloat16)


def width_weights(width):
    result = np.zeros((3, 2, 2 * width, 2 * width))
    for kind in range(3):
        cells = np.arange(-3, width + 3)
        full = np.array([[tap(c - x) for x in range(-1, width + 1)] for c in cells])
        if kind == 0:
            full[:3] = 0.0
            full[:, 0] = 0.0
        if kind == 2:
            full[-3:] = 0.0
            full[:, -1] = 0.0
        both = np.concatenate([full[:, 1:-1], 0.5 * (full[:, 2:] - full[:, :-2])], axis=1)
        for slot in range(2):
            result[kind, slot, :width] = both[3:-3]
            result[kind, slot, width + 4 * slot : width + 4 * slot + 3] = both[:3]
            result[kind, slot, width + 8 + 4 * slot : width + 8 + 4 * slot + 3] = both[-3:]
    return result.astype(ml_dtypes.bfloat16)


def edge_selector(width):
    result = np.zeros((16, 2 * width))
    for slot in range(2):
        for c in range(3):
            result[4 * slot + c, slot * width + width - 3 + c] = 1.0
            result[8 + 4 * slot + c, slot * width + c] = 1.0
    return result.astype(ml_dtypes.bfloat16)


def halves(values):
    high = values.astype(BF16)
    return high, (values - high.astype(F32)).astype(BF16)


def dot(a, b, dims=((1,), (0,))):
    return lax.dot_general(a, b, (dims, ((), ())), preferred_element_type=F32)


def kernel(
    n_gx, n_depth, cells_z,
    vol_hbm, ext_hbm, pal_hbm, pidx_hbm, zy_hbm, xw_hbm, sel_hbm,
    out_ref,
    vol, ext, pal, pidx, zy, xw, sel, tab,
    part, edge_out, edge_in, corner_in, z01_in, z23_in,
    beside, smooth, slope, piece_out, piece_in,
    load_sem, send_sem, recv_sem, piece_send, piece_recv, known_sem,
):
    gx = lax.axis_index("gx")
    me = lax.axis_index("depth")
    layers, height, width = vol.shape[1], vol.shape[2], vol.shape[3]
    has_left, has_right = gx > 0, gx < n_gx - 1
    has_near, has_far = me > 0, me < n_depth - 1

    kind = jnp.where(has_left, jnp.where(has_right, 1, 2), 0)
    loads = [
        pltpu.make_async_copy(vol_hbm.at[pl.ds(0, 2)], vol.at[pl.ds(0, 2)], load_sem.at[0]),
        pltpu.make_async_copy(zy_hbm, zy, load_sem.at[1]),
        pltpu.make_async_copy(vol_hbm.at[pl.ds(2, 2)], vol.at[pl.ds(2, 2)], load_sem.at[2]),
        pltpu.make_async_copy(sel_hbm, sel, load_sem.at[3]),
        pltpu.make_async_copy(xw_hbm.at[kind], xw, load_sem.at[4]),
        pltpu.make_async_copy(ext_hbm, ext, load_sem.at[5]),
        pltpu.make_async_copy(pal_hbm, pal, load_sem.at[6]),
        pltpu.make_async_copy(pidx_hbm, pidx, load_sem.at[7]),
    ]
    for load in loads[:2]:
        load.start()

    barrier = pltpu.get_barrier_semaphore()

    def around(distance):
        return lax.rem(me + n_depth + distance, n_depth)

    def greet(gx_to, depth_to, there):
        @pl.when(there)
        def _():
            pl.semaphore_signal(barrier, inc=1, device_id=(gx_to, depth_to), device_id_type=MESH)

    for step, there in ((1, has_far), (0, True)):
        greet(gx - 1, me + step, has_left & there)
        greet(gx + 1, me + step, has_right & there)
    reach = 4
    for distance in range(reach, 0, -1):
        for depth_to in (around(distance), around(-distance)):
            pl.semaphore_signal(barrier, inc=1, device_id=(gx, depth_to), device_id_type=MESH)
    for load in loads[2:]:
        load.start()

    @pl.when(me < FIRST)
    def _():
        @pl.loop(reach + 1, n_depth - reach)
        def _(distance):
            pl.semaphore_signal(
                barrier, inc=1, device_id=(gx, around(distance)), device_id_type=MESH
            )

    n_first = 0
    for device in range(FIRST):
        apart = lax.rem(me + n_depth - device, n_depth)
        n_first += ((apart > reach) & (apart < n_depth - reach)).astype(jnp.int32)

    def know():
        for depth_to in (around(reach), around(-reach)):
            pl.semaphore_signal(
                known_sem.at[reach.bit_length() - 3], inc=1, device_id=(gx, depth_to), device_id_type=MESH
            )

    def filter_own(pair):
        raw = jnp.concatenate(
            [vol[2 * pair + f].reshape(layers * height, width) for f in range(2)], axis=1
        )
        high, low = halves(raw)
        spread = dot(zy[...], high) + dot(zy[...], low)
        for f in range(2):
            part[2 * pair + f] = spread[:, f * width : (f + 1) * width].reshape(
                layers + 4, height, width
            )
        high, low = halves(spread)
        edges = dot(sel[...], high, ((1,), (1,))) + dot(sel[...], low, ((1,), (1,)))
        for side in range(2):
            for k in range(3):
                edge_out[side, k, pair] = edges[
                    8 * side : 8 * side + 8, 128 * k : 128 * k + 128
                ]

    for load in (loads[0], loads[1], loads[3]):
        load.wait()
    filter_own(0)
    loads[2].wait()
    filter_own(1)
    n_sides = has_left.astype(jnp.int32) + has_right.astype(jnp.int32)
    n_rows = 1 + has_near.astype(jnp.int32)
    pl.semaphore_wait(barrier, 2 * reach + n_sides * n_rows + n_first)
    know()

    table = [
        (edge_out.at[0, pl.ds(0, 2)], corner_in.at[0], gx + 1, me - 1, has_right & has_near, has_left & has_far),
        (edge_out.at[1, pl.ds(0, 2)], corner_in.at[1], gx - 1, me - 1, has_left & has_near, has_right & has_far),
        (edge_out.at[0], edge_in.at[0], gx + 1, me, has_right, has_left),
        (edge_out.at[1], edge_in.at[1], gx - 1, me, has_left, has_right),
    ]
    half = height // 2
    for h in range(2):
        rows = pl.ds(h * half, half)
        for fields, count, target in ((pl.ds(0, 2), 6, z01_in), (pl.ds(2, 2), 5, z23_in)):
            table.append(
                (part.at[fields, pl.ds(0, count), rows], target.at[h], gx, me - 1, has_near, has_far)
            )

    def copy(number):
        source, target, gx_to, depth_to = table[number][:4]
        return pltpu.make_async_remote_copy(
            src_ref=source,
            dst_ref=target,
            send_sem=send_sem.at[number],
            recv_sem=recv_sem.at[number],
            device_id=(gx_to, depth_to),
            device_id_type=MESH,
        )

    for number in range(len(table)):
        @pl.when(table[number][4])
        def _():
            copy(number).start()

    for _, target, _, _, _, comes in table:
        @pl.when(jnp.logical_not(comes))
        def _():
            target[...] = jnp.zeros(target.shape, F32)

    for load in loads[4:]:
        load.wait()

    step_len = 0.25 / cells_z
    colours = pal.shape[1]
    spread = jnp.concatenate([pal[...], jnp.zeros((3, 128 - colours), F32)], axis=1)
    chosen = jnp.broadcast_to(pidx[...], (8, 128))
    entries = [ext[...] * step_len] + [
        jnp.take_along_axis(
            jnp.broadcast_to(spread[c : c + 1], (8, 128)), chosen, axis=1, mode="promise_in_bounds"
        )[0:1]
        for c in range(3)
    ]
    entries = jnp.concatenate(entries, axis=0)
    tab[0:4] = entries
    tab[4:8] = jnp.concatenate([entries[:, 1:], entries[:, :1]], axis=1) - entries

    zeros8 = jnp.zeros((layers + 8, 8, width), F32)
    for f in range(2):
        smooth[f, :, 0:8] = zeros8
        smooth[f, :, height + 8 : height + 16] = zeros8

    while 2 * reach < n_depth // 2:
        pl.semaphore_wait(known_sem.at[reach.bit_length() - 3], 2)
        reach *= 2
        know()

    def arrived(*numbers):
        for number in numbers:
            @pl.when(table[number][5])
            def _():
                copy(number).wait_recv()

    keep_near = jnp.where(has_near, 1.0, 0.0).astype(F32)
    keep_far = jnp.where(has_far, 1.0, 0.0).astype(F32)

    def turn_edges(k):
        for pair in range(2):
            edge = jnp.zeros((16, 128), F32)
            if k < 3:
                edge += jnp.concatenate([edge_in[0, k, pair], edge_in[1, k, pair]], axis=0)
            if k >= 2:
                edge += jnp.concatenate(
                    [corner_in[0, k - 2, pair], corner_in[1, k - 2, pair]], axis=0
                )
            edge = jnp.transpose(jnp.concatenate([edge, jnp.zeros((112, 128), F32)], axis=0))
            beside[k, pair, 0], beside[k, pair, 1] = halves(edge)

    def filter_width(ks, start, size):
        ys = slice(start, start + size)
        blocks = [(k, pair) for k in ks for pair in range(2)]
        edges = [
            jnp.concatenate(
                [
                    beside[k, pair, i, 32 * j + start : 32 * j + start + size]
                    for k, pair in blocks
                    for j in range(4)
                ],
                axis=0,
            )
            for i in range(2)
        ]
        for f in range(2):
            body = []
            for k, pair in blocks:
                came, count = (z01_in, 6) if pair == 0 else (z23_in, 5)
                layer = []
                for j in range(4):
                    terms = []
                    if 4 * k + j < layers + 4:
                        terms.append(part[2 * pair + f, 4 * k + j, ys])
                    if 0 <= 4 * k + j - layers < count:
                        terms.append(came[start // half, f, 4 * k + j - layers])
                    layer.append(sum(terms) if terms else jnp.zeros((size, width), F32))
                body += layer
            own = halves(jnp.concatenate(body, axis=0))
            both = jnp.concatenate(
                [jnp.concatenate([own[i], edges[i]], axis=1) for i in range(2)], axis=0
            )
            found = dot(both, xw[f])
            found = found[: found.shape[0] // 2] + found[found.shape[0] // 2 :]
            for at, (k, pair) in enumerate(blocks):
                here = found[4 * size * at : 4 * size * (at + 1)]
                if pair == 0:
                    slope[f, 4 * k : 4 * k + 4, ys] = here[:, width:].reshape(4, size, width)
                here = here[:, :width].reshape(4, size, width)
                for j in range(4):
                    layer = here[j]
                    if pair == 0 and 4 * k + j == 1:
                        layer = layer * keep_near
                    if pair == 0 and 4 * k + j == layers + 2:
                        layer = layer * keep_far
                    smooth[2 * pair + f, 4 * k + j, 8 + start : 8 + start + size] = layer

    arrived(0, 1, 4, 5, 2, 3)
    for k in range(4):
        turn_edges(k)

    count = layers + 3
    top = ext.shape[1] - 1

    def look(row, at, fraction):
        def pick(r):
            entry = jnp.broadcast_to(tab[r : r + 1], (count * 8, 128))
            return jnp.take_along_axis(entry, at, axis=1, mode="promise_in_bounds")

        return (pick(row) + fraction * pick(row + 4)).reshape(count, 8, width)

    def piece(to):
        return pltpu.make_async_remote_copy(
            src_ref=piece_out.at[to],
            dst_ref=piece_in.at[me],
            send_sem=piece_send,
            recv_sem=piece_recv,
            device_id=(gx, to),
            device_id_type=MESH,
        )

    for t in range(height // 8):
        if t < 2:
            if t == 1:
                arrived(6, 7)
            filter_width((0, 1, 2, 3), half * t, half)
        here = pl.ds(8 * t + 8, 8)
        grads = []
        for f in range(2):
            grads.append(
                (
                    0.5 * (smooth[f, 3 : count + 3, here] - smooth[f, 1 : count + 1, here]),
                    0.5
                    * (
                        smooth[f, 2 : count + 2, 8 * t + 9 : 8 * t + 17]
                        - smooth[f, 2 : count + 2, 8 * t + 7 : 8 * t + 15]
                    ),
                    slope[f, 2 : count + 2, pl.ds(8 * t, 8)],
                )
            )
        z0, y0, x0 = grads[0]
        z1, y1, x1 = grads[1]
        facing = LIGHT[0] * z0 + LIGHT[1] * y0 + LIGHT[2] * x0
        steep = z0 * z0 + y0 * y0 + x0 * x0
        shading = 0.35 + 0.65 * facing * facing / (steep + 0.05)
        warm = z1 * z1 + y1 * y1 + x1 * x1
        gain = 0.25 + 1.5 * warm / (warm + 0.1)
        place = (0.5 * top) * (1.0 + jnp.tanh(smooth[0, 2 : count + 2, here]))
        at = jnp.clip(place.astype(jnp.int32), 0, top - 1)
        fraction = (place - at.astype(F32)).reshape(count * 8, width)
        at = at.reshape(count * 8, width)
        tau = look(0, at, fraction) * gain
        bright = (
            (1.0 + 0.5 * jnp.tanh(smooth[2, 2 : count + 2, here]))
            * jnp.exp(0.5 * jnp.tanh(smooth[3, 2 : count + 2, here]))
            * shading
        )
        absorbed = tau * (
            1.0
            - tau * (1 / 2)
            * (1.0 - tau * (1 / 3) * (1.0 - tau * (1 / 4) * (1.0 - tau * (1 / 5) * (1.0 - tau * (1 / 6)))))
        )
        opaque = jnp.zeros((8, width), F32)
        weights = []
        for z in range(count):
            here = absorbed[z]
            if z < 3:
                here = here * (1.0 - keep_near)
            if z >= layers:
                here = here * keep_far
            weight = here - here * opaque
            weights.append(weight[None])
            opaque = opaque + weight
        weight = jnp.concatenate(weights, axis=0) * bright
        for c in range(3):
            piece_out[pl.ds(8 * t, 8), c] = jnp.sum(weight * look(1 + c, at, fraction), axis=0)
        piece_out[pl.ds(8 * t, 8), 3] = opaque
        if t == 1:
            pl.semaphore_wait(known_sem.at[reach.bit_length() - 3], 2)

        @pl.loop(8 * t, 8 * t + 8)
        def _(to):
            @pl.when(to != me)
            def _():
                piece(to).start()

    own = pltpu.make_async_copy(piece_out.at[me], piece_in.at[me], piece_recv)
    own.start()
    for number in range(len(table)):
        @pl.when(table[number][4])
        def _():
            copy(number).wait_send()
    pltpu.make_async_copy(piece_in, piece_in, piece_recv).wait()
    others = piece_out.at[pl.ds(0, n_depth - 1)]
    pltpu.make_async_copy(others, others, piece_send).wait()

    group = n_depth // 8

    def over(nearer, farther):
        through = 1.0 - nearer[3]
        return [nearer[c] + through * farther[c] for c in range(4)]

    pieces = [
        [jnp.concatenate([piece_in[s * group + j, c : c + 1] for s in range(8)], axis=0) for c in range(4)]
        for j in range(group)
    ]
    total = pieces[0]
    for j in range(1, group):
        total = over(total, pieces[j])
    size = 8
    while size > 1:
        size //= 2
        nearer = [jnp.concatenate([v[2 * i : 2 * i + 1] for i in range(size)], axis=0) for v in total]
        farther = [jnp.concatenate([v[2 * i + 1 : 2 * i + 2] for i in range(size)], axis=0) for v in total]
        total = over(nearer, farther)
    out_ref[...] = jnp.concatenate(total, axis=0)


def solution(mesh):
    n_gx, n_depth = mesh.shape["gx"], mesh.shape["depth"]

    def per_device(volume, extinction, palette, palette_index):
        fields, layers, height, width = volume.shape
        entries = extinction.shape[0]
        colours = palette.shape[0]
        zy = depth_height_weights(layers, height)
        xw = width_weights(width)
        sel = edge_selector(width)
        anywhere = pl.BlockSpec(memory_space=pl.ANY)
        image = pl.pallas_call(
            functools.partial(kernel, n_gx, n_depth, layers * n_depth),
            out_shape=pltpu.VMEM((4, width), F32),
            in_specs=[anywhere] * 7,
            out_specs=pl.BlockSpec(memory_space=pltpu.VMEM),
            scratch_shapes=[
                pltpu.VMEM(volume.shape, F32),
                pltpu.VMEM((1, entries), F32),
                pltpu.VMEM((3, colours), F32),
                pltpu.VMEM((1, entries), jnp.int32),
                pltpu.VMEM(zy.shape, BF16),
                pltpu.VMEM(xw.shape[1:], BF16),
                pltpu.VMEM(sel.shape, BF16),
                pltpu.VMEM((8, entries), F32),
                pltpu.VMEM((fields, layers + 4, height, width), F32),
                pltpu.VMEM((2, 3, 2, 8, 128), F32),
                pltpu.VMEM((2, 3, 2, 8, 128), F32),
                pltpu.VMEM((2, 2, 2, 8, 128), F32),
                pltpu.VMEM((2, 2, 6, height // 2, width), F32),
                pltpu.VMEM((2, 2, 5, height // 2, width), F32),
                pltpu.VMEM((4, 2, 2, 128, 128), BF16),
                pltpu.VMEM((fields, layers + 8, height + 16, width), F32),
                pltpu.VMEM((2, layers + 8, height, width), F32),
                pltpu.VMEM((n_depth, 4, width), F32),
                pltpu.VMEM((n_depth, 4, width), F32),
                pltpu.SemaphoreType.DMA((8,)),
                pltpu.SemaphoreType.DMA((8,)),
                pltpu.SemaphoreType.DMA((8,)),
                pltpu.SemaphoreType.DMA,
                pltpu.SemaphoreType.DMA,
                pltpu.SemaphoreType.REGULAR((2,)),
            ],
            compiler_params=pltpu.CompilerParams(
                collective_id=0, has_side_effects=True, vmem_limit_bytes=VMEM_BYTES
            ),
        )(
            volume,
            extinction.reshape(1, entries),
            palette.T,
            palette_index.reshape(1, entries),
            jnp.asarray(zy),
            jnp.asarray(xw),
            jnp.asarray(sel),
        )
        return image.reshape(4, 1, width)

    placed = (P(None, "depth", None, "gx"), P(), P(), P())
    return jax.shard_map(
        per_device, mesh=mesh, in_specs=placed, out_specs=P(None, "gx", "depth"), check_vma=False
    )
```

```python
import functools

import jax
import jax.numpy as jnp
import ml_dtypes
import numpy as np
from jax import lax
from jax.experimental import pallas as pl
from jax.experimental.pallas import tpu as pltpu
from jax.sharding import PartitionSpec as P

TAPS = (0.0625, 0.25, 0.375, 0.25, 0.0625)
LIGHT = (0.64, 0.6, 0.48)
MESH = pl.DeviceIdType.MESH
FIRST = 8
VMEM_BYTES = 63 * 1024 * 1024
F32 = jnp.float32
BF16 = jnp.bfloat16


def tap(distance):
    return TAPS[distance + 2] if -2 <= distance <= 2 else 0.0


def depth_height_weights(layers, height):
    along_z = np.array([[tap(z - (i - 2)) for z in range(layers)] for i in range(layers + 4)])
    along_y = np.array([[tap(yy - y) for yy in range(height)] for y in range(height)])
    return np.kron(along_z, along_y).astype(ml_dtypes.bfloat16)


def width_weights(width):
    result = np.zeros((3, 2, 2 * width, 2 * width))
    for kind in range(3):
        cells = np.arange(-3, width + 3)
        full = np.array([[tap(c - x) for x in range(-1, width + 1)] for c in cells])
        if kind == 0:
            full[:3] = 0.0
            full[:, 0] = 0.0
        if kind == 2:
            full[-3:] = 0.0
            full[:, -1] = 0.0
        both = np.concatenate([full[:, 1:-1], 0.5 * (full[:, 2:] - full[:, :-2])], axis=1)
        for slot in range(2):
            result[kind, slot, :width] = both[3:-3]
            result[kind, slot, width + 4 * slot : width + 4 * slot + 3] = both[:3]
            result[kind, slot, width + 8 + 4 * slot : width + 8 + 4 * slot + 3] = both[-3:]
    return result.astype(ml_dtypes.bfloat16)


def edge_selector(width):
    result = np.zeros((16, 2 * width))
    for slot in range(2):
        for c in range(3):
            result[4 * slot + c, slot * width + width - 3 + c] = 1.0
            result[8 + 4 * slot + c, slot * width + c] = 1.0
    return result.astype(ml_dtypes.bfloat16)


def halves(values):
    high = values.astype(BF16)
    return high, (values - high.astype(F32)).astype(BF16)


def dot(a, b, dims=((1,), (0,))):
    return lax.dot_general(a, b, (dims, ((), ())), preferred_element_type=F32)


def kernel(
    n_gx, n_depth, cells_z,
    vol_hbm, ext_hbm, pal_hbm, pidx_hbm, zy_hbm, xw_hbm, sel_hbm,
    out_ref,
    vol, ext, pal, pidx, zy, xw, sel, tab,
    part, edge_out, edge_in, corner_in, z01_in, z23_in,
    beside, smooth, slope, piece_out, piece_in,
    load_sem, send_sem, recv_sem, piece_send, piece_recv, known_sem,
):
    gx = lax.axis_index("gx")
    me = lax.axis_index("depth")
    layers, height, width = vol.shape[1], vol.shape[2], vol.shape[3]
    has_left, has_right = gx > 0, gx < n_gx - 1
    has_near, has_far = me > 0, me < n_depth - 1

    kind = jnp.where(has_left, jnp.where(has_right, 1, 2), 0)
    loads = [
        pltpu.make_async_copy(vol_hbm.at[pl.ds(0, 2)], vol.at[pl.ds(0, 2)], load_sem.at[0]),
        pltpu.make_async_copy(zy_hbm, zy, load_sem.at[1]),
        pltpu.make_async_copy(vol_hbm.at[pl.ds(2, 2)], vol.at[pl.ds(2, 2)], load_sem.at[2]),
        pltpu.make_async_copy(sel_hbm, sel, load_sem.at[3]),
        pltpu.make_async_copy(xw_hbm.at[kind], xw, load_sem.at[4]),
        pltpu.make_async_copy(ext_hbm, ext, load_sem.at[5]),
        pltpu.make_async_copy(pal_hbm, pal, load_sem.at[6]),
        pltpu.make_async_copy(pidx_hbm, pidx, load_sem.at[7]),
    ]
    for load in loads[:2]:
        load.start()

    barrier = pltpu.get_barrier_semaphore()

    def around(distance):
        return lax.rem(me + n_depth + distance, n_depth)

    def greet(gx_to, depth_to, there):
        @pl.when(there)
        def _():
            pl.semaphore_signal(barrier, inc=1, device_id=(gx_to, depth_to), device_id_type=MESH)

    for step, there in ((1, has_far), (0, True)):
        greet(gx - 1, me + step, has_left & there)
        greet(gx + 1, me + step, has_right & there)
    reach = 4
    for distance in range(reach, 0, -1):
        for depth_to in (around(distance), around(-distance)):
            pl.semaphore_signal(barrier, inc=1, device_id=(gx, depth_to), device_id_type=MESH)
    for load in loads[2:]:
        load.start()

    @pl.when(me < FIRST)
    def _():
        @pl.loop(reach + 1, n_depth - reach)
        def _(distance):
            pl.semaphore_signal(
                barrier, inc=1, device_id=(gx, around(distance)), device_id_type=MESH
            )

    n_first = 0
    for device in range(FIRST):
        apart = lax.rem(me + n_depth - device, n_depth)
        n_first += ((apart > reach) & (apart < n_depth - reach)).astype(jnp.int32)

    def know():
        for depth_to in (around(reach), around(-reach)):
            pl.semaphore_signal(
                known_sem.at[reach.bit_length() - 3], inc=1, device_id=(gx, depth_to), device_id_type=MESH
            )

    def filter_own(pair):
        raw = jnp.concatenate(
            [vol[2 * pair + f].reshape(layers * height, width) for f in range(2)], axis=1
        )
        high, low = halves(raw)
        spread = dot(zy[...], high) + dot(zy[...], low)
        for f in range(2):
            part[2 * pair + f] = spread[:, f * width : (f + 1) * width].reshape(
                layers + 4, height, width
            )
        high, low = halves(spread)
        edges = dot(sel[...], high, ((1,), (1,))) + dot(sel[...], low, ((1,), (1,)))
        for side in range(2):
            for k in range(3):
                edge_out[side, k, pair] = edges[
                    8 * side : 8 * side + 8, 128 * k : 128 * k + 128
                ]

    for load in (loads[0], loads[1], loads[3]):
        load.wait()
    filter_own(0)
    loads[2].wait()
    filter_own(1)
    n_sides = has_left.astype(jnp.int32) + has_right.astype(jnp.int32)
    n_rows = 1 + has_near.astype(jnp.int32)
    pl.semaphore_wait(barrier, 2 * reach + n_sides * n_rows + n_first)
    know()

    left, right = lax.rem(gx + n_gx - 1, n_gx), lax.rem(gx + 1, n_gx)
    before = around(-1)
    table = [
        (edge_out.at[0, pl.ds(0, 2)], corner_in.at[0], right, before, has_right & has_near, has_left & has_far),
        (edge_out.at[1, pl.ds(0, 2)], corner_in.at[1], left, before, has_left & has_near, has_right & has_far),
        (edge_out.at[0], edge_in.at[0], right, me, has_right, has_left),
        (edge_out.at[1], edge_in.at[1], left, me, has_left, has_right),
    ]
    half = height // 2
    for h in range(2):
        rows = pl.ds(h * half, half)
        for fields, count, target in ((pl.ds(0, 2), 6, z01_in), (pl.ds(2, 2), 5, z23_in)):
            table.append(
                (part.at[fields, pl.ds(0, count), rows], target.at[h], gx, before, has_near, has_far)
            )

    def copy(number):
        source, target, gx_to, depth_to = table[number][:4]
        return pltpu.make_async_remote_copy(
            src_ref=source,
            dst_ref=target,
            send_sem=send_sem.at[number],
            recv_sem=recv_sem.at[number],
            device_id=(gx_to, depth_to),
            device_id_type=MESH,
        )

    for number in range(len(table)):
        @pl.when(table[number][4])
        def _():
            copy(number).start()

    for _, target, _, _, _, comes in table:
        @pl.when(jnp.logical_not(comes))
        def _():
            target[...] = jnp.zeros(target.shape, F32)

    for load in loads[4:]:
        load.wait()

    step_len = 0.25 / cells_z
    colours = pal.shape[1]
    spread = jnp.concatenate([pal[...], jnp.zeros((3, 128 - colours), F32)], axis=1)
    chosen = jnp.broadcast_to(pidx[...], (8, 128))
    entries = [ext[...] * step_len] + [
        jnp.take_along_axis(
            jnp.broadcast_to(spread[c : c + 1], (8, 128)), chosen, axis=1, mode="promise_in_bounds"
        )[0:1]
        for c in range(3)
    ]
    entries = jnp.concatenate(entries, axis=0)
    tab[0:4] = entries
    tab[4:8] = jnp.concatenate([entries[:, 1:], entries[:, :1]], axis=1) - entries

    zeros8 = jnp.zeros((layers + 8, 8, width), F32)
    for f in range(2):
        smooth[f, :, 0:8] = zeros8
        smooth[f, :, height + 8 : height + 16] = zeros8

    while 2 * reach < n_depth // 2:
        pl.semaphore_wait(known_sem.at[reach.bit_length() - 3], 2)
        reach *= 2
        know()

    def arrived(*numbers):
        for number in numbers:
            @pl.when(table[number][5])
            def _():
                copy(number).wait_recv()

    keep_near = jnp.where(has_near, 1.0, 0.0).astype(F32)
    keep_far = jnp.where(has_far, 1.0, 0.0).astype(F32)

    def turn_edges(k):
        for pair in range(2):
            edge = jnp.zeros((16, 128), F32)
            if k < 3:
                edge += jnp.concatenate([edge_in[0, k, pair], edge_in[1, k, pair]], axis=0)
            if k >= 2:
                edge += jnp.concatenate(
                    [corner_in[0, k - 2, pair], corner_in[1, k - 2, pair]], axis=0
                )
            edge = jnp.transpose(jnp.concatenate([edge, jnp.zeros((112, 128), F32)], axis=0))
            beside[k, pair, 0], beside[k, pair, 1] = halves(edge)

    def filter_width(ks, start, size):
        ys = slice(start, start + size)
        blocks = [(k, pair) for k in ks for pair in range(2)]
        edges = [
            jnp.concatenate(
                [
                    beside[k, pair, i, 32 * j + start : 32 * j + start + size]
                    for k, pair in blocks
                    for j in range(4)
                ],
                axis=0,
            )
            for i in range(2)
        ]
        for f in range(2):
            body = []
            for k, pair in blocks:
                came, count = (z01_in, 6) if pair == 0 else (z23_in, 5)
                layer = []
                for j in range(4):
                    terms = []
                    if 4 * k + j < layers + 4:
                        terms.append(part[2 * pair + f, 4 * k + j, ys])
                    if 0 <= 4 * k + j - layers < count:
                        terms.append(came[start // half, f, 4 * k + j - layers])
                    layer.append(sum(terms) if terms else jnp.zeros((size, width), F32))
                body += layer
            own = halves(jnp.concatenate(body, axis=0))
            both = jnp.concatenate(
                [jnp.concatenate([own[i], edges[i]], axis=1) for i in range(2)], axis=0
            )
            found = dot(both, xw[f])
            found = found[: found.shape[0] // 2] + found[found.shape[0] // 2 :]
            for at, (k, pair) in enumerate(blocks):
                here = found[4 * size * at : 4 * size * (at + 1)]
                if pair == 0:
                    slope[f, 4 * k : 4 * k + 4, ys] = here[:, width:].reshape(4, size, width)
                here = here[:, :width].reshape(4, size, width)
                for j in range(4):
                    layer = here[j]
                    if pair == 0 and 4 * k + j == 1:
                        layer = layer * keep_near
                    if pair == 0 and 4 * k + j == layers + 2:
                        layer = layer * keep_far
                    smooth[2 * pair + f, 4 * k + j, 8 + start : 8 + start + size] = layer

    arrived(0, 1, 4, 5, 2, 3)
    for k in range(4):
        turn_edges(k)

    count = layers + 3
    top = ext.shape[1] - 1

    def look(row, at, fraction):
        def pick(r):
            entry = jnp.broadcast_to(tab[r : r + 1], (count * 8, 128))
            return jnp.take_along_axis(entry, at, axis=1, mode="promise_in_bounds")

        return (pick(row) + fraction * pick(row + 4)).reshape(count, 8, width)

    def piece(to):
        return pltpu.make_async_remote_copy(
            src_ref=piece_out.at[to],
            dst_ref=piece_in.at[me],
            send_sem=piece_send,
            recv_sem=piece_recv,
            device_id=(gx, to),
            device_id_type=MESH,
        )

    for t in range(height // 8):
        if t < 2:
            if t == 1:
                arrived(6, 7)
            filter_width((0, 1, 2, 3), half * t, half)
        here = pl.ds(8 * t + 8, 8)
        grads = []
        for f in range(2):
            grads.append(
                (
                    0.5 * (smooth[f, 3 : count + 3, here] - smooth[f, 1 : count + 1, here]),
                    0.5
                    * (
                        smooth[f, 2 : count + 2, 8 * t + 9 : 8 * t + 17]
                        - smooth[f, 2 : count + 2, 8 * t + 7 : 8 * t + 15]
                    ),
                    slope[f, 2 : count + 2, pl.ds(8 * t, 8)],
                )
            )
        z0, y0, x0 = grads[0]
        z1, y1, x1 = grads[1]
        facing = LIGHT[0] * z0 + LIGHT[1] * y0 + LIGHT[2] * x0
        steep = z0 * z0 + y0 * y0 + x0 * x0
        shading = 0.35 + 0.65 * facing * facing / (steep + 0.05)
        warm = z1 * z1 + y1 * y1 + x1 * x1
        gain = 0.25 + 1.5 * warm / (warm + 0.1)
        place = (0.5 * top) * (1.0 + jnp.tanh(smooth[0, 2 : count + 2, here]))
        at = jnp.clip(place.astype(jnp.int32), 0, top - 1)
        fraction = (place - at.astype(F32)).reshape(count * 8, width)
        at = at.reshape(count * 8, width)
        tau = look(0, at, fraction) * gain
        bright = (
            (1.0 + 0.5 * jnp.tanh(smooth[2, 2 : count + 2, here]))
            * jnp.exp(0.5 * jnp.tanh(smooth[3, 2 : count + 2, here]))
            * shading
        )
        absorbed = tau * (
            1.0
            - tau * (1 / 2)
            * (1.0 - tau * (1 / 3) * (1.0 - tau * (1 / 4) * (1.0 - tau * (1 / 5) * (1.0 - tau * (1 / 6)))))
        )
        opaque = jnp.zeros((8, width), F32)
        weights = []
        for z in range(count):
            here = absorbed[z]
            if z < 3:
                here = here * (1.0 - keep_near)
            if z >= layers:
                here = here * keep_far
            weight = here - here * opaque
            weights.append(weight[None])
            opaque = opaque + weight
        weight = jnp.concatenate(weights, axis=0) * bright
        for c in range(3):
            piece_out[pl.ds(8 * t, 8), c] = jnp.sum(weight * look(1 + c, at, fraction), axis=0)
        piece_out[pl.ds(8 * t, 8), 3] = opaque
        if t == 1:
            pl.semaphore_wait(known_sem.at[reach.bit_length() - 3], 2)

        @pl.loop(8 * t, 8 * t + 8)
        def _(to):
            @pl.when(to != me)
            def _():
                piece(to).start()

    own = pltpu.make_async_copy(piece_out.at[me], piece_in.at[me], piece_recv)
    own.start()
    for number in range(len(table)):
        @pl.when(table[number][4])
        def _():
            copy(number).wait_send()
    pltpu.make_async_copy(piece_in, piece_in, piece_recv).wait()
    others = piece_out.at[pl.ds(0, n_depth - 1)]
    pltpu.make_async_copy(others, others, piece_send).wait()

    group = n_depth // 8

    def over(nearer, farther):
        through = 1.0 - nearer[3]
        return [nearer[c] + through * farther[c] for c in range(4)]

    pieces = [
        [jnp.concatenate([piece_in[s * group + j, c : c + 1] for s in range(8)], axis=0) for c in range(4)]
        for j in range(group)
    ]
    total = pieces[0]
    for j in range(1, group):
        total = over(total, pieces[j])
    size = 8
    while size > 1:
        size //= 2
        nearer = [jnp.concatenate([v[2 * i : 2 * i + 1] for i in range(size)], axis=0) for v in total]
        farther = [jnp.concatenate([v[2 * i + 1 : 2 * i + 2] for i in range(size)], axis=0) for v in total]
        total = over(nearer, farther)
    out_ref[...] = jnp.concatenate(total, axis=0)


def solution(mesh):
    n_gx, n_depth = mesh.shape["gx"], mesh.shape["depth"]

    def per_device(volume, extinction, palette, palette_index):
        fields, layers, height, width = volume.shape
        entries = extinction.shape[0]
        colours = palette.shape[0]
        zy = depth_height_weights(layers, height)
        xw = width_weights(width)
        sel = edge_selector(width)
        anywhere = pl.BlockSpec(memory_space=pl.ANY)
        image = pl.pallas_call(
            functools.partial(kernel, n_gx, n_depth, layers * n_depth),
            out_shape=pltpu.VMEM((4, width), F32),
            in_specs=[anywhere] * 7,
            out_specs=pl.BlockSpec(memory_space=pltpu.VMEM),
            scratch_shapes=[
                pltpu.VMEM(volume.shape, F32),
                pltpu.VMEM((1, entries), F32),
                pltpu.VMEM((3, colours), F32),
                pltpu.VMEM((1, entries), jnp.int32),
                pltpu.VMEM(zy.shape, BF16),
                pltpu.VMEM(xw.shape[1:], BF16),
                pltpu.VMEM(sel.shape, BF16),
                pltpu.VMEM((8, entries), F32),
                pltpu.VMEM((fields, layers + 4, height, width), F32),
                pltpu.VMEM((2, 3, 2, 8, 128), F32),
                pltpu.VMEM((2, 3, 2, 8, 128), F32),
                pltpu.VMEM((2, 2, 2, 8, 128), F32),
                pltpu.VMEM((2, 2, 6, height // 2, width), F32),
                pltpu.VMEM((2, 2, 5, height // 2, width), F32),
                pltpu.VMEM((4, 2, 2, 128, 128), BF16),
                pltpu.VMEM((fields, layers + 8, height + 16, width), F32),
                pltpu.VMEM((2, layers + 8, height, width), F32),
                pltpu.VMEM((n_depth, 4, width), F32),
                pltpu.VMEM((n_depth, 4, width), F32),
                pltpu.SemaphoreType.DMA((8,)),
                pltpu.SemaphoreType.DMA((8,)),
                pltpu.SemaphoreType.DMA((8,)),
                pltpu.SemaphoreType.DMA,
                pltpu.SemaphoreType.DMA,
                pltpu.SemaphoreType.REGULAR((2,)),
            ],
            compiler_params=pltpu.CompilerParams(
                collective_id=0, has_side_effects=True, vmem_limit_bytes=VMEM_BYTES
            ),
        )(
            volume,
            extinction.reshape(1, entries),
            palette.T,
            palette_index.reshape(1, entries),
            jnp.asarray(zy),
            jnp.asarray(xw),
            jnp.asarray(sel),
        )
        return image.reshape(4, 1, width)

    placed = (P(None, "depth", None, "gx"), P(), P(), P())
    return jax.shard_map(
        per_device, mesh=mesh, in_specs=placed, out_specs=P(None, "gx", "depth"), check_vma=False
    )
```
